256 devices in a mesh: src: 16 (over x, y_lo, core), tgt: 16 (over z, y_hi).
Axes of the slice: x: 4, y: 4 (y_hi: 2, y_lo: 2; y = y_hi * 2 + y_lo), z: 8, core: 2. Of those that a mesh axis runs over, the one named last changes fastest.
Arguments:
- src_feat: bfloat16 [32768, 256], P(('src', 'tgt')), may hold values from -90 to 90
- tgt_feat: bfloat16 [32768, 256], P(('tgt', 'src')), may hold values from -30 to 30
- src_weight: float32 [32768], P('src'), may hold values from 0.2 to 5
- tgt_weight: float32 [32768], P('tgt'), may hold values from 0.2 to 5
- cand: int32 [256, 16, 6], P('src', 'tgt'), may hold values from 0 to 15, as said below
- counts: int32 [256, 16], P('src', 'tgt'), may hold values from 1 to 6, as said below
Outputs:
- src_potential: float32 [32768], P('src')
- tgt_potential: float32 [32768], P('tgt')
The draws below stay inside these ranges and needn't reach their ends.
Inputs may be any that keep to these rules, and one draw needn't show every extreme that they name: For each source block b and target shard t the entries cand[b, t, k] with k < counts[b, t] name distinct blocks, and cand[b, t, 0] equals b modulo 16; slots from counts[b, t] on are not used. `counts`: 6 is reached in every draw.
All inputs are finite; a program needn't handle non-finite values.
Results may differ from the reference program's by a relative error of at most 0.0003.
Values may be sent and summed in bfloat16 or wider, within the bound.
No kernel may reach another device: no remote copies, remote signals or barrier semaphores. Data moves between devices by JAX's collectives and lax.ppermute only.
A program may use at most 64 MiB of HBM per device.

```python
import math
import jax
import jax.numpy as jnp
from jax import lax

F = 256
BLK = 128
KC = 6
ITERS = 3
PB = 16
SBLOCKS = 256
NS = 32768
NT = 32768
N_SRC = 16
N_TGT = 16


def shared_normals(key):
    return jnp.clip(jax.random.normal(key, (NT, F), jnp.float32), -6.0, 6.0)


def draw_tgt_feat(key, part):
    values = shared_normals(key)
    return values.astype(jnp.bfloat16)


def draw_src_feat(key, part):
    key = jax.random.fold_in(key, 5)
    first_key = jax.random.fold_in(key, 0)
    values = jnp.clip(jax.random.normal(first_key, (NS, F), jnp.float32), -6.0, 6.0)
    return values.astype(jnp.bfloat16)


def draw_cand(key, part):
    key = jax.random.fold_in(key, 41)
    width = PB - 1
    scores = jax.random.randint(key, (SBLOCKS, N_TGT, width), 0, 1 << 20) * width
    scores = scores + jnp.arange(width, dtype=jnp.int32)[None, None, :]
    offsets = jnp.argsort(scores, axis=-1)[:, :, :KC - 1].astype(jnp.int32) + 1
    offsets = jnp.concatenate([jnp.zeros((SBLOCKS, N_TGT, 1), jnp.int32), offsets], axis=-1)
    block_ids = jnp.arange(SBLOCKS, dtype=jnp.int32)[:, None, None]
    return ((block_ids + offsets) % PB).astype(jnp.int32)


def draw_counts(key, part):
    key = jax.random.fold_in(key, 31)
    first_key, second_key, third_key = jax.random.split(key, 3)
    limit = jax.random.randint(first_key, (N_SRC, 1, N_TGT), 2, KC + 1)
    raw_draw = jax.random.randint(second_key, (N_SRC, PB, N_TGT), 0, KC)
    values = (1 + raw_draw % limit).reshape(SBLOCKS, N_TGT)
    chosen = jax.random.randint(third_key, (), 0, SBLOCKS * N_TGT)
    flat_ids = jnp.arange(SBLOCKS * N_TGT, dtype=jnp.int32).reshape(SBLOCKS, N_TGT)
    return jnp.where(flat_ids == chosen, KC, values).astype(jnp.int32)


def steps_of(stream_key, extent, pieces, smallest, high):
    def one(axis_at, parts):
        steps = jax.random.uniform(jax.random.fold_in(jax.random.fold_in(stream_key, 6), axis_at), (parts,), jnp.float32, smallest / len(pieces), high / len(pieces))
        return jnp.repeat(jnp.exp(steps), extent[axis_at] // parts).reshape((-1,) + (1,) * (len(extent) - axis_at - 1))

    gain = one(*pieces[0])
    for cut in pieces[1:]:
        gain = gain * one(*cut)
    return gain


def setup_inputs(seed: int = 0) -> dict:
    keys = jax.random.split(jax.random.key(seed), 7)
    return {
        "src_feat": draw_src_feat(jax.random.fold_in(keys[6], 71), 0),
        "tgt_feat": draw_tgt_feat(jax.random.fold_in(keys[6], 71), 0),
        "src_weight": jnp.clip(jnp.exp(math.log(5.0) - 3.218876 * jax.random.uniform(keys[2], (NS,), jnp.float32) ** steps_of(keys[2], (NS,), ((0, 16),), -0.2, 0.2)), 0.2, 5.0),
        "tgt_weight": jnp.clip(jnp.exp(math.log(5.0) - 3.218876 * jax.random.uniform(keys[3], (NT,), jnp.float32) ** steps_of(keys[3], (NT,), ((0, 16),), -0.2, 0.2)), 0.2, 5.0),
        "cand": draw_cand(jax.random.fold_in(keys[6], 71), 0),
        "counts": draw_counts(jax.random.fold_in(keys[6], 71), 0),
    }


def reference(src_feat, tgt_feat, src_weight, tgt_weight, cand, counts):
    source_blocks = PB * N_SRC
    target_blocks = PB * N_TGT
    scale = 1.0 / math.sqrt(F)
    shard_ids = jnp.arange(N_TGT, dtype=jnp.int32)
    global_ids = (shard_ids[None, :, None] * PB + cand).reshape(source_blocks, N_TGT * KC).astype(jnp.int32)
    usable = (jnp.arange(KC, dtype=jnp.int32)[None, None, :] < counts[:, :, None]).reshape(source_blocks, N_TGT * KC)
    source_tiles = src_feat.reshape(source_blocks, BLK, F)
    target_tiles = tgt_feat.reshape(target_blocks, BLK, F)
    block_list = jnp.arange(source_blocks, dtype=jnp.int32)

    def scores_of(which):
        left_rows = source_tiles[which].astype(jnp.float32)
        right_rows = target_tiles[global_ids[which]].astype(jnp.float32)
        return jnp.einsum('rf,kcf->rkc', left_rows, right_rows, precision=lax.Precision.HIGHEST) * scale

    def row_pass(target_dual):
        tiles = target_dual.reshape(target_blocks, BLK)

        def one_block(which):
            shifted = jnp.where(usable[which][None, :, None], scores_of(which) + tiles[global_ids[which]][None, :, :], -jnp.inf)
            highest = lax.optimization_barrier(jnp.max(shifted, axis=(1, 2)))
            totals = lax.optimization_barrier(jnp.sum(jnp.exp(shifted - highest[:, None, None]), axis=(1, 2)))
            return (highest, totals)
        highest, totals = lax.map(one_block, block_list)
        return jnp.log(src_weight) - (highest.reshape(-1) + jnp.log(totals.reshape(-1)))

    def column_pass(source_dual):
        tiles = source_dual.reshape(source_blocks, BLK)

        def one_block(which):
            shifted = jnp.where(usable[which][None, :, None], scores_of(which) + tiles[which][:, None, None], -jnp.inf)
            highest = lax.optimization_barrier(jnp.max(shifted, axis=0))
            safe_high = jnp.where(usable[which][:, None], highest, 0.0)
            totals = lax.optimization_barrier(jnp.sum(jnp.exp(shifted - safe_high[None, :, :]), axis=0))
            return (jnp.where(usable[which][:, None], highest, -jnp.inf), totals)
        highest, totals = lax.map(one_block, block_list)
        flat_ids = global_ids.reshape(-1)
        flat_high = highest.reshape(-1, BLK)
        highest_all = jnp.full((target_blocks, BLK), -jnp.inf, jnp.float32).at[flat_ids].max(flat_high)
        flat_usable = usable.reshape(-1)[:, None]
        shifted_high = jnp.where(flat_usable, flat_high, 0.0) - highest_all[flat_ids]
        terms = jnp.where(flat_usable, totals.reshape(-1, BLK) * jnp.exp(shifted_high), 0.0)
        summed = jax.ops.segment_sum(terms, flat_ids, num_segments=target_blocks)
        return jnp.log(tgt_weight) - (highest_all.reshape(-1) + jnp.log(summed.reshape(-1)))
    target_dual = jnp.zeros((target_blocks * BLK,), jnp.float32)
    source_dual = jnp.zeros((source_blocks * BLK,), jnp.float32)
    for iteration in range(ITERS):
        source_dual = row_pass(target_dual)
        target_dual = column_pass(source_dual)
    return (source_dual, target_dual)
```

```python
import functools
import math

import jax
import jax.numpy as jnp
from jax import lax
from jax.experimental import pallas as pl
from jax.experimental.pallas import tpu as pltpu
from jax.sharding import PartitionSpec as P

ITERS = 3
UNROLL = 2
LOW = -1e30
LN2 = math.log(2.0)
LOG2E = math.log2(math.e)

VMEM = pl.BlockSpec(memory_space=pltpu.VMEM)
SMEM = pl.BlockSpec(memory_space=pltpu.SMEM)
PARAMS = pltpu.CompilerParams(vmem_limit_bytes=24 * 1024 * 1024)


def plan_kernel(blocks, slots, targets, room, cand_ref, counts_ref, plan_ref):
    spare = blocks * targets
    total = 0
    for block in range(blocks):

        def add(slot, at, block=block):
            target = cand_ref[block * slots + slot]
            plan_ref[at] = block
            plan_ref[room + at] = target
            plan_ref[2 * room + at] = target * blocks + block
            plan_ref[3 * room + at] = block * targets + target
            return at + 1

        total = lax.fori_loop(0, counts_ref[block], add, total)
    for extra in range(UNROLL):
        plan_ref[total + extra] = 0
        plan_ref[room + total + extra] = 0
        plan_ref[2 * room + total + extra] = spare
        plan_ref[3 * room + total + extra] = spare
    plan_ref[4 * room] = (total + UNROLL - 1) // UNROLL


def clear(high_ref, total_ref):
    high_ref[...] = jnp.full(high_ref.shape, LOW, jnp.float32)
    total_ref[...] = jnp.zeros(total_ref.shape, jnp.float32)


def keep_stats(shifted, row, high_ref, total_ref):
    highest = jnp.max(shifted, axis=0, keepdims=True)
    high_ref[pl.ds(row, 1), :] = highest
    total_ref[pl.ds(row, 1), :] = jnp.sum(jnp.exp2(shifted - highest), axis=0, keepdims=True)


def combine(high, total):
    highest = jnp.max(high, axis=0)
    return highest, jnp.sum(total * jnp.exp2(high - highest[None]), axis=0)


def send_out(high_ref, total_ref, kept, out_ref):
    outer = (high_ref.shape[0] - 8) // kept
    shape = (outer, kept, high_ref.shape[1])
    high = high_ref[: outer * kept, :].reshape(shape)
    total = total_ref[: outer * kept, :].reshape(shape)
    highest, totals = combine(high, total)
    local = highest + jnp.log2(totals)
    for part in range(out_ref.shape[0]):
        out_ref[part] = local


def potential(parts_ref, weight_ref):
    parts = parts_ref[...]
    highest = jnp.max(parts, axis=0)
    totals = jnp.sum(jnp.exp2(parts - highest[None]), axis=0)
    return jnp.log2(weight_ref[...]) - (highest + jnp.log2(totals))


def first_kernel(room, scale, plan_ref, src_ref, tgt_ref, scores_ref, flipped_ref, out_ref,
                 high_ref, total_ref):
    clear(high_ref, total_ref)
    contract = (((1,), (1,)), ((), ()))

    def group(step, carry):
        for lane in range(UNROLL):
            at = step * UNROLL + lane
            left = src_ref[plan_ref[at]]
            right = tgt_ref[plan_ref[room + at]]
            scores_ref[at] = scale * lax.dot_general(
                left, right, contract, preferred_element_type=jnp.float32)
            flipped = scale * lax.dot_general(
                right, left, contract, preferred_element_type=jnp.float32)
            flipped_ref[at] = flipped
            keep_stats(flipped, plan_ref[2 * room + at], high_ref, total_ref)
        return carry

    lax.fori_loop(0, plan_ref[4 * room], group, 0)
    send_out(high_ref, total_ref, src_ref.shape[0], out_ref)


def pass_kernel(room, own, row, kept, emit, plan_ref, parts_ref, weight_ref, scores_ref, out_ref,
                *refs):
    if emit:
        dual_ref, refs = refs[0], refs[1:]
    column_ref, high_ref, total_ref = refs
    dual = potential(parts_ref, weight_ref)
    if emit:
        dual_ref[...] = dual * LN2
    turned = dual.T
    for block in range(column_ref.shape[0]):
        column_ref[block] = jnp.broadcast_to(turned[:, block : block + 1], column_ref.shape[1:])
    clear(high_ref, total_ref)

    def group(step, carry):
        for lane in range(UNROLL):
            at = step * UNROLL + lane
            shifted = scores_ref[at] + column_ref[plan_ref[own * room + at]]
            keep_stats(shifted, plan_ref[row * room + at], high_ref, total_ref)
        return carry

    lax.fori_loop(0, plan_ref[4 * room], group, 0)
    send_out(high_ref, total_ref, kept, out_ref)


def last_kernel(parts_ref, weight_ref, dual_ref):
    dual_ref[...] = potential(parts_ref, weight_ref) * LN2


def spread(rows, axis):
    whole = jnp.broadcast_to(rows[None], (lax.axis_size(axis),) + rows.shape)
    return lax.all_to_all(whole, axis, 0, 0)


def on_device(src_feat, tgt_feat, src_weight, tgt_weight, cand, counts):
    blocks, _, slots = cand.shape
    size = src_feat.shape[0]
    targets = lax.axis_size("src")
    features = src_feat.shape[1]
    pairs = blocks * slots
    room = -(-(pairs + UNROLL) // 128) * 128
    held = -(-pairs // UNROLL) * UNROLL
    src_weight = src_weight.reshape(blocks, size)
    tgt_weight = tgt_weight.reshape(targets, size)

    plan = pl.pallas_call(
        functools.partial(plan_kernel, blocks, slots, targets, room),
        out_shape=jax.ShapeDtypeStruct((5 * room,), jnp.int32),
        in_specs=[SMEM, SMEM],
        out_specs=SMEM,
        name="plan",
    )(cand.reshape(-1), counts.reshape(-1))

    with jax.named_scope("gather_features"):
        source_rows = spread(src_feat, "tgt")
        target_rows = spread(tgt_feat, "src")

    tables = [pltpu.VMEM((blocks * targets + 8, size), jnp.float32)] * 2
    tile_shape = (held, size, size)
    to_tgt = jax.ShapeDtypeStruct((lax.axis_size("tgt"), blocks, size), jnp.float32)
    to_src = jax.ShapeDtypeStruct((lax.axis_size("src"), targets, size), jnp.float32)

    scores, flipped, parts = pl.pallas_call(
        functools.partial(first_kernel, room, LOG2E / math.sqrt(features)),
        out_shape=(pltpu.VMEM(tile_shape, jnp.float32), pltpu.VMEM(tile_shape, jnp.float32), to_tgt),
        in_specs=[SMEM, VMEM, VMEM],
        out_specs=(VMEM, VMEM, VMEM),
        scratch_shapes=tables,
        compiler_params=PARAMS,
        name="scores_and_rows",
    )(plan, source_rows, target_rows)

    def sweep(own, row, kept, emit, parts, weight, tiles, out, name):
        shapes = (out,) + ((jax.ShapeDtypeStruct(weight.shape, jnp.float32),) if emit else ())
        return pl.pallas_call(
            functools.partial(pass_kernel, room, own, row, kept, emit),
            out_shape=shapes,
            in_specs=[SMEM, VMEM, VMEM, VMEM],
            out_specs=(VMEM,) * len(shapes),
            scratch_shapes=[pltpu.VMEM((weight.shape[0], size, size), jnp.float32)] + tables,
            compiler_params=PARAMS,
            name=name,
        )(plan, parts, weight, pltpu.with_memory_space_constraint(tiles, pltpu.VMEM))

    for step in range(ITERS):
        if step:
            (parts,) = sweep(1, 2, blocks, False, parts, tgt_weight, flipped, to_tgt, "rows")
        with jax.named_scope("exchange_rows"):
            parts = lax.all_to_all(parts, "tgt", 0, 0)
        last = step == ITERS - 1
        parts, *source_dual = sweep(0, 3, targets, last, parts, src_weight, scores, to_src, "columns")
        with jax.named_scope("exchange_columns"):
            parts = lax.all_to_all(parts, "src", 0, 0)
    target_dual = pl.pallas_call(
        last_kernel,
        out_shape=jax.ShapeDtypeStruct((targets, size), jnp.float32),
        in_specs=[VMEM, VMEM],
        out_specs=VMEM,
        name="last",
    )(parts, tgt_weight)
    return (source_dual[0].reshape(-1), target_dual.reshape(-1))


def solution(mesh):
    placed = (
        P(("src", "tgt"), None),
        P(("tgt", "src"), None),
        P("src"),
        P("tgt"),
        P("src", "tgt", None),
        P("src", "tgt"),
    )
    return jax.shard_map(
        on_device, mesh=mesh, in_specs=placed, out_specs=(P("src"), P("tgt")), check_vma=False
    )
```

```python
import functools
import math

import jax
import jax.numpy as jnp
from jax import lax
from jax.experimental import pallas as pl
from jax.experimental.pallas import tpu as pltpu
from jax.sharding import PartitionSpec as P

ITERS = 3
UNROLL = 2
FIELDS = 5
LOW = -1e30
LN2 = math.log(2.0)
LOG2E = math.log2(math.e)

VMEM = pl.BlockSpec(memory_space=pltpu.VMEM)
SMEM = pl.BlockSpec(memory_space=pltpu.SMEM)
PARAMS = pltpu.CompilerParams(vmem_limit_bytes=8 * 1024 * 1024)


def plan_kernel(blocks, slots, targets, room, cand_ref, counts_ref, plan_ref):
    spare = blocks * targets
    here = lax.axis_index("tgt")
    deep, side = here // 2, here % 2
    stages = blocks // 2

    def put(at, block, target, row, column, place):
        for field, value in enumerate((block, target, row, column, place)):
            plan_ref[field * room + at] = value

    total = 0
    for chunk, offset in enumerate(arrival(stages)):
        plan_ref[FIELDS * room + chunk] = total // UNROLL
        for place in range(2):
            block = ((deep + offset + stages) % stages) * 2 + (side + place) % 2

            def add(slot, at, block=block, place=place):
                target = cand_ref[block * slots + slot]
                put(at, block, target, target * blocks + block, block * targets + target, place)
                return at + 1

            total = lax.fori_loop(0, counts_ref[block], add, total)
        for extra in range(UNROLL - 1):
            put(total + extra, 0, 0, spare, spare, 0)
        total = (total + UNROLL - 1) // UNROLL * UNROLL
    plan_ref[FIELDS * room + stages] = total // UNROLL


def arrival(stages):
    offsets = [0]
    for hop in range(1, stages // 2):
        offsets += [-hop, hop]
    return offsets + [stages // 2]


def clear(high_ref, total_ref):
    high_ref[...] = jnp.full(high_ref.shape, LOW, jnp.float32)
    total_ref[...] = jnp.zeros(total_ref.shape, jnp.float32)


def keep_stats(shifted, row, high_ref, total_ref):
    highest = jnp.max(shifted, axis=0, keepdims=True)
    high_ref[pl.ds(row, 1), :] = highest
    total_ref[pl.ds(row, 1), :] = jnp.sum(jnp.exp2(shifted - highest), axis=0, keepdims=True)


def combine(high, total):
    highest = jnp.max(high, axis=0)
    return highest, jnp.sum(total * jnp.exp2(high - highest[None]), axis=0)


def local_lse(high_ref, total_ref, kept):
    outer = (high_ref.shape[0] - 8) // kept
    shape = (outer, kept, high_ref.shape[1])
    high = high_ref[: outer * kept, :].reshape(shape)
    total = total_ref[: outer * kept, :].reshape(shape)
    highest, totals = combine(high, total)
    return highest + jnp.log2(totals)


def copies(local, out_ref):
    for part in range(out_ref.shape[0]):
        out_ref[part] = local


def potential(parts_ref, weight_ref):
    parts = parts_ref[...]
    highest = jnp.max(parts, axis=0)
    totals = jnp.sum(jnp.exp2(parts - highest[None]), axis=0)
    return jnp.log2(weight_ref[...]) - (highest + jnp.log2(totals))


def matmul(left, right, scale):
    return scale * lax.dot_general(
        left, right, (((1,), (1,)), ((), ())), preferred_element_type=jnp.float32)


def over_pairs(plan_ref, room, first, chunks, body):
    for chunk, ref in enumerate(chunks, first):

        def group(step, carry, ref=ref):
            for lane in range(UNROLL):
                body(ref, step * UNROLL + lane)
            return carry

        bounds = FIELDS * room + chunk
        lax.fori_loop(plan_ref[bounds], plan_ref[bounds + 1], group, 0)


def cost(pairs):
    return pl.CostEstimate(flops=pairs * 2 * 128 * 128 * 256, bytes_accessed=pairs * 65536, transcendentals=0)


def first_kernel(room, scale, first, count, plan_ref, tgt_ref, *refs):
    chunks, refs = refs[:count], refs[count:]
    if first:
        earlier_ref, refs = refs[0], refs[3:]
    flipped_ref, scores_ref, out_ref, high_ref, total_ref = refs
    clear(high_ref, total_ref)

    def body(ref, at):
        left, right = ref[plan_ref[4 * room + at]], tgt_ref[plan_ref[room + at]]
        flipped = matmul(right, left, scale)
        flipped_ref[at] = flipped
        scores_ref[at] = matmul(left, right, scale)
        keep_stats(flipped, plan_ref[2 * room + at], high_ref, total_ref)

    over_pairs(plan_ref, room, first, chunks, body)
    local = local_lse(high_ref, total_ref, out_ref.shape[-2])
    if first:
        local = jnp.maximum(local, earlier_ref[...])
    if len(out_ref.shape) == 3:
        copies(local, out_ref)
    else:
        out_ref[...] = local


def pass_kernel(room, column_chunks, own, row, kept, emit, plan_ref, parts_ref, weight_ref, scores_ref, out_ref,
                *refs):
    if emit:
        dual_ref, refs = refs[0], refs[1:]
    column_ref, high_ref, total_ref = refs
    dual = potential(parts_ref, weight_ref)
    if emit:
        dual_ref[...] = dual * LN2
    turned = dual.T
    for block in range(column_ref.shape[0]):
        column_ref[block] = jnp.broadcast_to(turned[:, block : block + 1], column_ref.shape[1:])
    clear(high_ref, total_ref)

    def group(step, carry):
        for lane in range(UNROLL):
            at = step * UNROLL + lane
            shifted = scores_ref[at] + column_ref[plan_ref[own * room + at]]
            keep_stats(shifted, plan_ref[row * room + at], high_ref, total_ref)
        return carry

    lax.fori_loop(0, plan_ref[FIELDS * room + column_chunks], group, 0)
    copies(local_lse(high_ref, total_ref, kept), out_ref)


def last_kernel(parts_ref, weight_ref, dual_ref):
    dual_ref[...] = potential(parts_ref, weight_ref) * LN2


def spread(rows, axis):
    whole = jnp.broadcast_to(rows[None], (lax.axis_size(axis),) + rows.shape)
    return lax.all_to_all(whole, axis, 0, 0)


def ring(rows, beside):
    size = lax.axis_size("tgt")
    stages = size // 2

    def along_z(value, by):
        return lax.ppermute(
            value, "tgt", [(k, (k // 2 + by) % stages * 2 + k % 2) for k in range(size)])

    other = lax.ppermute(rows, "tgt", [(k, k ^ 1) for k in range(size)])
    own = jnp.stack([rows, other])
    up, down, chunks = own, own, [own]
    for hop in range(1, stages // 2):
        if hop == stages // 2 - 1:
            up, down, beside = lax.optimization_barrier((up, down, beside))
        up, down = along_z(up, 1), along_z(down, -1)
        chunks += [up, down]

    def last(before):
        ends = lax.optimization_barrier((up[0], down[1], before))
        return jnp.stack([along_z(ends[0], 1), along_z(ends[1], -1)]), ends[2]

    return chunks, last, beside


def on_device(src_feat, tgt_feat, src_weight, tgt_weight, cand, counts):
    blocks, _, slots = cand.shape
    size, features = src_feat.shape
    targets = lax.axis_size("src")
    stages = blocks // 2
    held = blocks * slots + stages * UNROLL
    room = -(-held // 128) * 128
    src_weight = src_weight.reshape(blocks, size)
    tgt_weight = tgt_weight.reshape(targets, size)

    plan = pl.pallas_call(
        functools.partial(plan_kernel, blocks, slots, targets, room),
        out_shape=pltpu.SMEM(((FIELDS + 1) * room,), jnp.int32),
        in_specs=[SMEM, SMEM],
        out_specs=SMEM,
        compiler_params=PARAMS,
        name="plan",
    )(cand.reshape(-1), counts.reshape(-1))
    plan = pltpu.with_memory_space_constraint(plan, pltpu.SMEM)

    with jax.named_scope("gather_features"):
        target_rows = spread(tgt_feat, "src")
        chunks, last_chunk, target_rows = ring(src_feat, target_rows)

    tables = [pltpu.VMEM((blocks * targets + 8, size), jnp.float32)] * 2
    tiles = pltpu.VMEM((held, size, size), jnp.float32)
    to_tgt = jax.ShapeDtypeStruct((lax.axis_size("tgt"), blocks, size), jnp.float32)
    to_src = jax.ShapeDtypeStruct((lax.axis_size("src"), targets, size), jnp.float32)
    scale = LOG2E / math.sqrt(features)

    def first_rows(first, some, local, scored, out, pairs, name):
        kept = [pltpu.with_memory_space_constraint(part, pltpu.VMEM) for part in scored]
        more = [local] + kept if scored else []
        given = 2 + len(some)
        *scored, local = pl.pallas_call(
            functools.partial(first_kernel, room, scale, first, len(some)),
            out_shape=(tiles, tiles, out),
            in_specs=[SMEM] + [VMEM] * (1 + len(some) + len(more)),
            out_specs=(VMEM, VMEM, VMEM),
            scratch_shapes=tables,
            input_output_aliases={given + 1: 0, given + 2: 1} if more else {},
            compiler_params=PARAMS,
            cost_estimate=cost(pairs),
            name=name,
        )(plan, target_rows, *some, *more)
        return scored, local

    one = jax.ShapeDtypeStruct((blocks, size), jnp.float32)
    split = len(chunks) - 2
    scored, local = first_rows(0, chunks[:split], None, (), one, 26, "rows_early")
    end, local = last_chunk(local)
    scored, local = first_rows(split, chunks[split:], local, scored, one, 12, "rows_middle")
    (flipped, scores), parts = first_rows(split + 2, [end], local, scored, to_tgt, 6, "rows_late")

    def sweep(own, row, kept, emit, parts, weight, tiles, out, name):
        shapes = (out,) + ((jax.ShapeDtypeStruct(weight.shape, jnp.float32),) if emit else ())
        return pl.pallas_call(
            functools.partial(pass_kernel, room, stages, own, row, kept, emit),
            out_shape=shapes,
            in_specs=[SMEM, VMEM, VMEM, VMEM],
            out_specs=(VMEM,) * len(shapes),
            scratch_shapes=[pltpu.VMEM((weight.shape[0], size, size), jnp.float32)] + tables,
            compiler_params=PARAMS,
            name=name,
        )(plan, parts, weight, pltpu.with_memory_space_constraint(tiles, pltpu.VMEM))

    for step in range(ITERS):
        if step:
            (parts,) = sweep(1, 2, blocks, False, parts, tgt_weight, flipped, to_tgt, "rows")
        with jax.named_scope("exchange_rows"):
            parts = lax.all_to_all(parts, "tgt", 0, 0)
        last = step == ITERS - 1
        parts, *source_dual = sweep(0, 3, targets, last, parts, src_weight, scores, to_src, "columns")
        with jax.named_scope("exchange_columns"):
            parts = lax.all_to_all(parts, "src", 0, 0)
    target_dual = pl.pallas_call(
        last_kernel,
        out_shape=jax.ShapeDtypeStruct((targets, size), jnp.float32),
        in_specs=[VMEM, VMEM],
        out_specs=VMEM,
        compiler_params=PARAMS,
        name="last",
    )(parts, tgt_weight)
    return (source_dual[0].reshape(-1), target_dual.reshape(-1))


def solution(mesh):
    placed = (
        P(("src", "tgt"), None),
        P(("tgt", "src"), None),
        P("src"),
        P("tgt"),
        P("src", "tgt", None),
        P("src", "tgt"),
    )
    return jax.shard_map(
        on_device, mesh=mesh, in_specs=placed, out_specs=(P("src"), P("tgt")), check_vma=False
    )
```

```python
import functools
import math

import jax
import jax.numpy as jnp
from jax import lax
from jax.experimental import pallas as pl
from jax.experimental.pallas import tpu as pltpu
from jax.sharding import PartitionSpec as P

ITERS = 3
UNROLL = 4
FIELDS = 5
LOW = -1e30
LN2 = math.log(2.0)
LOG2E = math.log2(math.e)

VMEM = pl.BlockSpec(memory_space=pltpu.VMEM)
SMEM = pl.BlockSpec(memory_space=pltpu.SMEM)
PARAMS = pltpu.CompilerParams(vmem_limit_bytes=8 * 1024 * 1024)


def plan_kernel(blocks, slots, targets, room, cand_ref, counts_ref, src_ref, tgt_ref, plan_ref,
                src_log_ref, tgt_log_ref):
    src_log_ref[...] = jnp.log2(src_ref[...])
    tgt_log_ref[...] = jnp.log2(tgt_ref[...])
    spare = blocks * targets
    here = lax.axis_index("tgt")
    deep, side = here // 2, here % 2
    stages = blocks // 2

    def put(at, block, target, row, column, place):
        for field, value in enumerate((block, target, row, column, place)):
            plan_ref[field * room + at] = value

    total = 0
    for chunk, offset in enumerate(arrival(stages)):
        plan_ref[FIELDS * room + chunk] = total // UNROLL
        for place in range(2):
            block = ((deep + offset + stages) % stages) * 2 + (side + place) % 2

            def add(slot, at, block=block, place=place):
                target = cand_ref[block * slots + slot]
                put(at, block, target, target * blocks + block, block * targets + target, place)
                return at + 1

            total = lax.fori_loop(0, counts_ref[block], add, total)
        for extra in range(UNROLL - 1):
            put(total + extra, 0, 0, spare, spare, 0)
        total = (total + UNROLL - 1) // UNROLL * UNROLL
    plan_ref[FIELDS * room + stages] = total // UNROLL


def arrival(stages):
    offsets = [0]
    for hop in range(1, stages // 2):
        offsets += [-hop, hop]
    return offsets + [stages // 2]


def clear(high_ref, total_ref):
    high_ref[...] = jnp.full(high_ref.shape, LOW, jnp.float32)
    total_ref[...] = jnp.zeros(total_ref.shape, jnp.float32)


def keep_stats(shifted, row, high_ref, total_ref):
    highest = jnp.max(shifted, axis=0, keepdims=True)
    high_ref[pl.ds(row, 1), :] = highest
    total_ref[pl.ds(row, 1), :] = jnp.sum(jnp.exp2(shifted - highest), axis=0, keepdims=True)


def combine(high, total):
    highest = jnp.max(high, axis=0)
    return highest, jnp.sum(total * jnp.exp2(high - highest[None]), axis=0)


def local_lse(high_ref, total_ref, kept):
    outer = (high_ref.shape[0] - 8) // kept
    shape = (outer, kept, high_ref.shape[1])
    high = high_ref[: outer * kept, :].reshape(shape)
    total = total_ref[: outer * kept, :].reshape(shape)
    highest, totals = combine(high, total)
    return highest + jnp.log2(totals)


def copies(local, out_ref):
    for part in range(out_ref.shape[0]):
        out_ref[part] = local


def potential(parts_ref, weight_ref):
    parts = parts_ref[...]
    highest = jnp.max(parts, axis=0)
    totals = jnp.sum(jnp.exp2(parts - highest[None]), axis=0)
    return weight_ref[...] - (highest + jnp.log2(totals))


def matmul(left, right, scale):
    return scale * lax.dot_general(
        left, right, (((1,), (1,)), ((), ())), preferred_element_type=jnp.float32)


def over_pairs(plan_ref, room, first, chunks, body):
    for chunk, ref in enumerate(chunks, first):

        def group(step, carry, ref=ref):
            for lane in range(UNROLL):
                body(ref, step * UNROLL + lane)
            return carry

        bounds = FIELDS * room + chunk
        lax.fori_loop(plan_ref[bounds], plan_ref[bounds + 1], group, 0)


def cost(pairs):
    return pl.CostEstimate(flops=pairs * 2 * 128 * 128 * 256, bytes_accessed=pairs * 65536, transcendentals=0)


def first_kernel(room, scale, first, count, plan_ref, tgt_ref, *refs):
    chunks, refs = refs[:count], refs[count:]
    if first:
        earlier_ref, refs = refs[0], refs[3:]
    flipped_ref, scores_ref, out_ref, high_ref, total_ref = refs
    clear(high_ref, total_ref)

    def body(ref, at):
        left, right = ref[plan_ref[4 * room + at]], tgt_ref[plan_ref[room + at]]
        flipped = matmul(right, left, scale)
        flipped_ref[at] = flipped
        scores_ref[at] = matmul(left, right, scale)
        keep_stats(flipped, plan_ref[2 * room + at], high_ref, total_ref)

    over_pairs(plan_ref, room, first, chunks, body)
    local = local_lse(high_ref, total_ref, out_ref.shape[-2])
    if first:
        local = jnp.maximum(local, earlier_ref[...])
    if len(out_ref.shape) == 3:
        copies(local, out_ref)
    else:
        out_ref[...] = local


def pass_kernel(room, column_chunks, own, row, kept, emit, plan_ref, parts_ref, weight_ref, scores_ref, out_ref,
                *refs):
    if emit:
        dual_ref, refs = refs[0], refs[1:]
    column_ref, high_ref, total_ref = refs
    dual = potential(parts_ref, weight_ref)
    if emit:
        dual_ref[...] = dual * LN2
    turned = dual.T
    for block in range(column_ref.shape[0]):
        column_ref[block] = jnp.broadcast_to(turned[:, block : block + 1], column_ref.shape[1:])
    clear(high_ref, total_ref)

    def group(step, carry):
        for lane in range(UNROLL):
            at = step * UNROLL + lane
            shifted = scores_ref[at] + column_ref[plan_ref[own * room + at]]
            keep_stats(shifted, plan_ref[row * room + at], high_ref, total_ref)
        return carry

    lax.fori_loop(0, plan_ref[FIELDS * room + column_chunks], group, 0)
    copies(local_lse(high_ref, total_ref, kept), out_ref)


def last_kernel(parts_ref, weight_ref, dual_ref):
    dual_ref[...] = potential(parts_ref, weight_ref) * LN2


def ring(rows, beside):
    size = lax.axis_size("tgt")
    stages = size // 2

    def along_z(value, by):
        return lax.ppermute(
            value, "tgt", [(k, (k // 2 + by) % stages * 2 + k % 2) for k in range(size)])

    other = lax.ppermute(rows, "tgt", [(k, k ^ 1) for k in range(size)])
    whole = jnp.broadcast_to(beside[0][None], (lax.axis_size("src"),) + beside[0].shape)
    whole, weight, other = lax.optimization_barrier((whole, beside[1], other))
    beside = lax.all_to_all(whole, "src", 0, 0), weight
    own = jnp.stack([rows, other])
    up, down, chunks = own, own, [own]
    for hop in range(1, stages // 2):
        if hop == stages // 2 - 1:
            up, down, beside = lax.optimization_barrier((up, down, beside))
        up, down = along_z(up, 1), along_z(down, -1)
        chunks += [up, down]

    def last(before):
        ends = lax.optimization_barrier((up[0], down[1], before))
        return jnp.stack([along_z(ends[0], 1), along_z(ends[1], -1)]), ends[2]

    return chunks, last, beside


def on_device(src_feat, tgt_feat, src_weight, tgt_weight, cand, counts):
    blocks, _, slots = cand.shape
    size, features = src_feat.shape
    targets = lax.axis_size("src")
    stages = blocks // 2
    held = blocks * slots + stages * UNROLL
    room = -(-held // 128) * 128
    src_weight = src_weight.reshape(blocks, size)
    tgt_weight = tgt_weight.reshape(targets, size)

    plan, src_weight, tgt_weight = pl.pallas_call(
        functools.partial(plan_kernel, blocks, slots, targets, room),
        out_shape=(
            pltpu.SMEM(((FIELDS + 1) * room,), jnp.int32),
            jax.ShapeDtypeStruct(src_weight.shape, jnp.float32),
            jax.ShapeDtypeStruct(tgt_weight.shape, jnp.float32),
        ),
        in_specs=[SMEM, SMEM, VMEM, VMEM],
        out_specs=(SMEM, VMEM, VMEM),
        compiler_params=PARAMS,
        name="plan",
    )(cand.reshape(-1), counts.reshape(-1), src_weight, tgt_weight)
    plan = pltpu.with_memory_space_constraint(plan, pltpu.SMEM)

    with jax.named_scope("gather_features"):
        chunks, last_chunk, target_rows = ring(src_feat, (tgt_feat, src_weight))
        target_rows, src_weight = target_rows

    tables = [pltpu.VMEM((blocks * targets + 8, size), jnp.float32)] * 2
    tiles = pltpu.VMEM((held, size, size), jnp.float32)
    to_tgt = jax.ShapeDtypeStruct((lax.axis_size("tgt"), blocks, size), jnp.float32)
    to_src = jax.ShapeDtypeStruct((lax.axis_size("src"), targets, size), jnp.float32)
    scale = LOG2E / math.sqrt(features)

    def first_rows(first, some, local, scored, out, pairs, name):
        kept = [pltpu.with_memory_space_constraint(part, pltpu.VMEM) for part in scored]
        more = [local] + kept if scored else []
        given = 2 + len(some)
        *scored, local = pl.pallas_call(
            functools.partial(first_kernel, room, scale, first, len(some)),
            out_shape=(tiles, tiles, out),
            in_specs=[SMEM] + [VMEM] * (1 + len(some) + len(more)),
            out_specs=(VMEM, VMEM, VMEM),
            scratch_shapes=tables,
            input_output_aliases={given + 1: 0, given + 2: 1} if more else {},
            compiler_params=PARAMS,
            cost_estimate=cost(pairs),
            name=name,
        )(plan, target_rows, *some, *more)
        return scored, local

    one = jax.ShapeDtypeStruct((blocks, size), jnp.float32)
    split = len(chunks) - 2
    scored, local = first_rows(0, chunks[:split], None, (), one, 26, "rows_early")
    end, local = last_chunk(local)
    scored, local = first_rows(split, chunks[split:], local, scored, one, 12, "rows_middle")
    (flipped, scores), parts = first_rows(split + 2, [end], local, scored, to_tgt, 6, "rows_late")

    def sweep(own, row, kept, emit, parts, weight, tiles, out, name):
        shapes = (out,) + ((jax.ShapeDtypeStruct(weight.shape, jnp.float32),) if emit else ())
        return pl.pallas_call(
            functools.partial(pass_kernel, room, stages, own, row, kept, emit),
            out_shape=shapes,
            in_specs=[SMEM, VMEM, VMEM, VMEM],
            out_specs=(VMEM,) * len(shapes),
            scratch_shapes=[pltpu.VMEM((weight.shape[0], size, size), jnp.float32)] + tables,
            compiler_params=PARAMS,
            name=name,
        )(plan, parts, weight, pltpu.with_memory_space_constraint(tiles, pltpu.VMEM))

    for step in range(ITERS):
        if step:
            (parts,) = sweep(1, 2, blocks, False, parts, tgt_weight, flipped, to_tgt, "rows")
        with jax.named_scope("exchange_rows"):
            parts = lax.all_to_all(parts, "tgt", 0, 0)
        last = step == ITERS - 1
        parts, *source_dual = sweep(0, 3, targets, last, parts, src_weight, scores, to_src, "columns")
        with jax.named_scope("exchange_columns"):
            parts = lax.all_to_all(parts, "src", 0, 0)
    target_dual = pl.pallas_call(
        last_kernel,
        out_shape=jax.ShapeDtypeStruct((targets, size), jnp.float32),
        in_specs=[VMEM, VMEM],
        out_specs=VMEM,
        compiler_params=PARAMS,
        name="last",
    )(parts, tgt_weight)
    return (source_dual[0].reshape(-1), target_dual.reshape(-1))


def solution(mesh):
    placed = (
        P(("src", "tgt"), None),
        P(("tgt", "src"), None),
        P("src"),
        P("tgt"),
        P("src", "tgt", None),
        P("src", "tgt"),
    )
    return jax.shard_map(
        on_device, mesh=mesh, in_specs=placed, out_specs=(P("src"), P("tgt")), check_vma=False
    )
```

```python
import functools
import math

import jax
import jax.numpy as jnp
from jax import lax
from jax.experimental import pallas as pl
from jax.experimental.pallas import tpu as pltpu
from jax.sharding import Mesh
from jax.sharding import PartitionSpec as P

ITERS = 3
UNROLL = 8
FIELDS = 5
LOW = -1e30
LN2 = math.log(2.0)
LOG2E = math.log2(math.e)

SRC = {"x": 4, "l": 2, "c": 2}
TGT = {"z": 8, "h": 2}
ROW_GROUP = ("z", "c")
COLUMN_GROUP = ("x", "l", "h")
LAST_GROUP = ("x", "l", "c", "h")
PIECES = (8,)

VMEM = pl.BlockSpec(memory_space=pltpu.VMEM)
SMEM = pl.BlockSpec(memory_space=pltpu.SMEM)
ANY = pl.BlockSpec(memory_space=pl.ANY)
PARAMS = pltpu.CompilerParams(vmem_limit_bytes=8 * 1024 * 1024)


def arrival(stages):
    offsets = [0]
    for hop in range(1, stages // 2):
        offsets += [-hop, hop]
    return offsets + [stages // 2]


def prepare_kernel(slots, own_hbm, tgt_hbm, *refs):
    lists_hbm, whole_ref, held_ref, tgt_ref, info_ref, refs, sems = refs[:4], *refs[4:8], refs[8:-1], refs[-1]
    pairs = ((tgt_hbm, tgt_ref), (own_hbm, held_ref)) + tuple(zip(lists_hbm, refs))
    moves = [pltpu.make_async_copy(source, target, sems.at[n]) for n, (source, target) in enumerate(pairs)]
    for move in moves:
        move.start()
    info_ref[...] = jnp.zeros(info_ref.shape, jnp.float32)
    for move in moves:
        move.wait()
    for flip, (cand_ref, counts_ref) in enumerate((refs[:2], refs[2:])):
        blocks = cand_ref.shape[2]
        for slot in range(slots):
            info_ref[8 * flip + slot : 8 * flip + slot + 1, :blocks] = cand_ref[slot].astype(jnp.float32)
        info_ref[8 * flip + slots : 8 * flip + slots + 1, :blocks] = counts_ref[...].astype(jnp.float32)
    size = tgt_ref.shape[0]
    info = info_ref[...].astype(whole_ref.dtype)
    for part in range(whole_ref.shape[0]):
        whole_ref[part, :size, :] = tgt_ref[...]
        whole_ref[part, size:, :] = info


def plan_kernel(stages, slots, room, rows_ref, src_hbm, tgt_hbm, plan_ref, src_log_ref, tgt_log_ref, src_ref,
                tgt_ref, lists_ref, info_ref, sems):
    moves = (pltpu.make_async_copy(src_hbm, src_ref, sems.at[0]), pltpu.make_async_copy(tgt_hbm, tgt_ref, sems.at[1]))
    for move in moves:
        move.start()
    deep, side, core = lax.axis_index("z"), lax.axis_index("h"), lax.axis_index("c")
    pair = (lax.axis_index("x") * 2 + lax.axis_index("l")) * 2
    lanes = lists_ref.shape[1]
    size = rows_ref.shape[1] - 16
    for flip in range(2):
        rows = rows_ref[pair + (side + flip) % 2, size:, :lanes].astype(jnp.float32)
        lists_ref[16 * flip : 16 * flip + 16, :] = rows.astype(jnp.int32)
    fetch = pltpu.make_async_copy(lists_ref, info_ref, sems.at[2])
    fetch.start()
    fetch.wait()
    blocks = 2 * stages
    spare = blocks * blocks

    def put(at, block, target, row, column, place):
        for field, value in enumerate((block, target, row, column, place)):
            plan_ref[field * room + at] = value

    total = 0
    offsets = arrival(stages)
    chunk = 0
    for piece, length in enumerate(PIECES):
        plan_ref[FIELDS * room + piece] = total // UNROLL
        for place in range(2 * length):
            depth = (deep + offsets[chunk + place // 2] + stages) % stages
            first = 8 * (place % 2)
            block = depth * 2 + (core + place % 2) % 2
            row = depth * 2 + side
            for flip in range(2):

                def add(slot, at, first=first, flip=flip, row=row, block=block, place=place):
                    local = info_ref[16 * flip + first + slot, row]
                    target = local - local % 2 + (side + flip) % 2
                    put(at, block, target, target * blocks + block, block * blocks + target, place)
                    return at + jnp.where(local % 2 == core, 1, 0)

                total = lax.fori_loop(0, info_ref[16 * flip + first + slots, row], add, total)
        for extra in range(UNROLL - 1):
            put(total + extra, 0, 0, spare, spare, 0)
        total = (total + UNROLL - 1) // UNROLL * UNROLL
        chunk += length
    plan_ref[FIELDS * room + len(PIECES)] = total // UNROLL
    for move in moves:
        move.wait()
    for row in range(stages):
        src_log_ref[row : row + 1, :] = jnp.log2(src_ref[pl.ds(row * 2 + side, 1), :])
        tgt_log_ref[row : row + 1, :] = jnp.log2(tgt_ref[pl.ds(row * 2 + core, 1), :])


def clear(high_ref, total_ref):
    high_ref[...] = jnp.full(high_ref.shape, LOW, jnp.float32)
    total_ref[...] = jnp.zeros(total_ref.shape, jnp.float32)


def keep_stats(shifted, row, high_ref, total_ref):
    highest = jnp.max(shifted, axis=0, keepdims=True)
    high_ref[pl.ds(row, 1), :] = highest
    total_ref[pl.ds(row, 1), :] = jnp.sum(jnp.exp2(shifted - highest), axis=0, keepdims=True)


def local_lse(high_ref, total_ref, kept):
    outer = (high_ref.shape[0] - 8) // kept
    shape = (outer, kept, high_ref.shape[1])
    high = high_ref[: outer * kept, :].reshape(shape)
    total = total_ref[: outer * kept, :].reshape(shape)
    highest = jnp.max(high, axis=0)
    totals = jnp.sum(total * jnp.exp2(high - highest[None]), axis=0)
    return highest + jnp.log2(totals)


def copies(local, log_ref, out_ref):
    kept = local.shape[0]
    for part in range(out_ref.shape[0]):
        out_ref[part, :kept, :] = local
        if log_ref is not None:
            out_ref[part, kept:, :] = log_ref[...]


def potential(parts_ref, weight):
    parts = parts_ref[:, : weight.shape[0], :]
    highest = jnp.max(parts, axis=0)
    totals = jnp.sum(jnp.exp2(parts - highest[None]), axis=0)
    return weight - (highest + jnp.log2(totals))


def matmul(left, right, scale):
    return scale * lax.dot_general(
        left, right, (((1,), (1,)), ((), ())), preferred_element_type=jnp.float32)


def first_kernel(room, scale, piece, plan_ref, tgt_ref, *refs):
    count = 2 * PIECES[piece]
    features, refs = refs[:count], refs[count:]
    log_ref = earlier_ref = None
    if piece:
        earlier_ref, refs = refs[0], refs[3:]
    if piece == len(PIECES) - 1:
        log_ref, refs = refs[0], refs[1:]
    flipped_ref, scores_ref, out_ref, held_ref, high_ref, total_ref = refs
    for place, ref in enumerate(features):
        held_ref[place] = ref[...]
    clear(high_ref, total_ref)

    def group(step, carry):
        for lane in range(UNROLL):
            at = step * UNROLL + lane
            left, right = held_ref[plan_ref[4 * room + at]], tgt_ref[plan_ref[room + at], : held_ref.shape[1], :]
            flipped = matmul(right, left, scale)
            flipped_ref[at] = flipped
            scores_ref[at] = matmul(left, right, scale)
            keep_stats(flipped, plan_ref[2 * room + at], high_ref, total_ref)
        return carry

    bounds = FIELDS * room + piece
    lax.fori_loop(plan_ref[bounds], plan_ref[bounds + 1], group, 0)
    local = local_lse(high_ref, total_ref, out_ref.shape[0])
    if piece:
        local = jnp.maximum(local, earlier_ref[...])
    if log_ref is None:
        out_ref[...] = local
    else:
        copies(local, log_ref, out_ref)


def pass_kernel(room, own, row, fresh, first, emit, plan_ref, parts_ref, weight_ref, scores_ref, *refs):
    log_ref = weight_ref if first else None
    out_ref, refs = refs[0], refs[1:]
    if fresh:
        kept_ref, refs = refs[0], refs[1:]
        blocks = kept_ref.shape[0]
        for block in range(blocks):
            at = blocks + block // 2
            kept_ref[block : block + 1, :] = parts_ref[block % 2, at : at + 1, :]
        weight_ref = kept_ref
    if emit:
        dual_ref, refs = refs[0], refs[1:]
    column_ref, high_ref, total_ref = refs
    dual = potential(parts_ref, weight_ref[...])
    blocks = dual.shape[0]
    if emit:
        high_ref[:blocks, :] = dual * LN2
        for block in range(blocks // 2):
            dual_ref[block : block + 1, :] = high_ref[pl.ds(2 * block + lax.axis_index("c"), 1), :]
    turned = dual.T
    for block in range(blocks):
        column_ref[block] = jnp.broadcast_to(turned[:, block : block + 1], column_ref.shape[1:])
    clear(high_ref, total_ref)

    def group(step, carry):
        for lane in range(UNROLL):
            at = step * UNROLL + lane
            shifted = scores_ref[at] + column_ref[plan_ref[own * room + at]]
            keep_stats(shifted, plan_ref[row * room + at], high_ref, total_ref)
        return carry

    lax.fori_loop(0, plan_ref[FIELDS * room + len(PIECES)], group, 0)
    local = local_lse(high_ref, total_ref, blocks)
    if not emit:
        copies(local, log_ref, out_ref)
        return
    for block in range(blocks):
        at = block % 2 * (blocks // 2) + block // 2
        high_ref[at : at + 1, :] = local[block : block + 1, :]
    for part in range(out_ref.shape[0]):
        out_ref[part] = high_ref[pl.ds(part % 2 * (blocks // 2), blocks // 2), :]


def interleave(out_ref, axis, mine_ref, other_ref):
    side = lax.axis_index(axis)
    for block in range(mine_ref.shape[0]):
        out_ref[pl.ds(2 * block + side, 1), :] = mine_ref[block : block + 1, :]
        out_ref[pl.ds(2 * block + 1 - side, 1), :] = other_ref[block : block + 1, :]


def last_kernel(parts_ref, weight_ref, mine_ref, other_ref, src_ref, tgt_ref, lse_ref):
    interleave(src_ref, "h", mine_ref, other_ref)
    for core in range(2):
        parts = [parts_ref[part] for part in range(parts_ref.shape[0]) if part // 2 % 2 == core]
        highest = functools.reduce(jnp.maximum, parts)
        lse = highest + jnp.log2(sum(jnp.exp2(part - highest) for part in parts))
        for block in range(lse.shape[0]):
            at = 2 * block + core
            lse_ref[at : at + 1, :] = lse[block : block + 1, :]
    tgt_ref[...] = (jnp.log2(weight_ref[...]) - lse_ref[...]) * LN2


def cost(pairs):
    return pl.CostEstimate(flops=pairs * 2 * 128 * 128 * 256, bytes_accessed=pairs * 65536, transcendentals=0)


def in_hbm(value):
    return pltpu.with_memory_space_constraint(value, pltpu.HBM)


def swap(value, axis):
    return lax.ppermute(value, axis, [(0, 1), (1, 0)])


def along_z(value, by):
    stages = lax.axis_size("z")
    return lax.ppermute(value, "z", [(k, (k + by) % stages) for k in range(stages)])


def on_device(src_feat, tgt_feat, src_weight, tgt_weight, cand, counts):
    slots = cand.shape[2]
    size, features = src_feat.shape
    stages = lax.axis_size("z")
    blocks = 2 * stages
    held = -(-2 * blocks * slots // UNROLL) * UNROLL + len(PIECES) * UNROLL
    room = -(-held // 128) * 128
    scale = LOG2E / math.sqrt(features)

    lists = (cand.transpose(2, 1, 0), counts.T)
    across = tuple(swap(part, "c") for part in lists)
    whole, own = pl.pallas_call(
        functools.partial(prepare_kernel, slots),
        out_shape=(
            jax.ShapeDtypeStruct((blocks, size + 16, features), tgt_feat.dtype),
            pltpu.VMEM(src_feat.shape, src_feat.dtype),
        ),
        in_specs=[ANY] * 6,
        out_specs=(VMEM, VMEM),
        scratch_shapes=[pltpu.VMEM(tgt_feat.shape, tgt_feat.dtype), pltpu.VMEM((16, features), jnp.float32)]
        + [pltpu.VMEM((slots, 1, blocks), jnp.int32), pltpu.VMEM((1, blocks), jnp.int32)] * 2
        + [pltpu.SemaphoreType.DMA((6,))],
        compiler_params=PARAMS,
        name="prepare",
    )(in_hbm(src_feat), in_hbm(tgt_feat), *map(in_hbm, lists), *across)
    with jax.named_scope("gather_features"):
        gated = (swap(src_feat, "c"), along_z(src_feat, 1), along_z(src_feat, -1))
        whole, other, up, down = lax.optimization_barrier((whole, *gated))
        target_rows = lax.all_to_all(whole, COLUMN_GROUP, 0, 0)
        chunks = [src_feat, up, down]
        for _ in range(2, stages // 2):
            up, down = along_z(up, 1), along_z(down, -1)
            chunks += [up, down]
        chunks += [along_z(up, 1)]
        pairs = [own, other] + [part for chunk in chunks[1:] for part in (chunk, swap(chunk, "c"))]

    half = jax.ShapeDtypeStruct((stages, size), jnp.float32)
    plan, src_log, tgt_log = pl.pallas_call(
        functools.partial(plan_kernel, stages, slots, room),
        out_shape=(pltpu.SMEM(((FIELDS + 1) * room,), jnp.int32), half, half),
        in_specs=[VMEM] + [ANY] * 2,
        out_specs=(SMEM, VMEM, VMEM),
        scratch_shapes=[pltpu.VMEM((blocks, size), jnp.float32)] * 2
        + [pltpu.VMEM((32, size), jnp.int32), pltpu.SMEM((32, size), jnp.int32), pltpu.SemaphoreType.DMA((3,))],
        compiler_params=PARAMS,
        name="plan",
    )(target_rows, in_hbm(src_weight.reshape(blocks, size)), in_hbm(tgt_weight.reshape(blocks, size)))
    plan = pltpu.with_memory_space_constraint(plan, pltpu.SMEM)

    tables = [pltpu.VMEM((blocks * blocks + 8, size), jnp.float32)] * 2
    tiles = pltpu.VMEM((held, size, size), jnp.float32)
    whole_rows = jax.ShapeDtypeStruct((blocks, size), jnp.float32)
    parts_of = lambda kept: jax.ShapeDtypeStruct((blocks, kept, size), jnp.float32)

    def first_rows(piece, some, local, scored, out, log, name):
        kept = [pltpu.with_memory_space_constraint(part, pltpu.VMEM) for part in scored]
        more = ([local] + kept if scored else []) + log
        given = 2 + len(some)
        *scored, local = pl.pallas_call(
            functools.partial(first_kernel, room, scale, piece),
            out_shape=(tiles, tiles, out),
            in_specs=[SMEM] + [VMEM] * (1 + len(some) + len(more)),
            out_specs=(VMEM, VMEM, VMEM),
            scratch_shapes=[pltpu.VMEM((len(some), size, features), src_feat.dtype)] + tables,
            input_output_aliases={given + 1: 0, given + 2: 1} if scored else {},
            compiler_params=PARAMS,
            cost_estimate=cost(5 * PIECES[piece]),
            name=name,
        )(plan, target_rows, *some, *more)
        return scored, local

    (flipped, scores), parts = first_rows(0, pairs, None, (), parts_of(blocks + stages), [src_log], "scores_and_rows")

    def sweep(own, row, step, emit, parts, weight, tiles, name):
        first, fresh = name == "columns" and not step, weight is None
        shapes = (parts_of(blocks + stages if first else blocks),)
        if emit:
            shapes = (jax.ShapeDtypeStruct((2 * blocks, stages, size), jnp.float32),)
        shapes += (whole_rows,) * fresh + (half,) * emit
        weights = tgt_log if fresh else weight
        return pl.pallas_call(
            functools.partial(pass_kernel, room, own, row, fresh, first, emit),
            out_shape=shapes,
            in_specs=[SMEM, VMEM, VMEM, VMEM],
            out_specs=(VMEM,) * len(shapes),
            scratch_shapes=[pltpu.VMEM((blocks, size, size), jnp.float32)] + tables,
            compiler_params=PARAMS,
            name=name,
        )(plan, parts, weights, pltpu.with_memory_space_constraint(tiles, pltpu.VMEM))

    src_kept = tgt_kept = None
    for step in range(ITERS):
        if step:
            parts, *kept = sweep(1, 2, step, False, parts, tgt_kept, flipped, "rows")
            tgt_kept = kept[0] if kept else tgt_kept
        with jax.named_scope("exchange_rows"):
            parts = lax.all_to_all(parts, ROW_GROUP, 0, 0)
        last = step == ITERS - 1
        parts, *kept = sweep(0, 3, step, last, parts, src_kept, scores, "columns")
        if last:
            mine = kept.pop()
            other = swap(mine, "h")
        src_kept = kept[0] if kept else src_kept
        with jax.named_scope("exchange_columns"):
            parts = lax.all_to_all(parts, LAST_GROUP if last else COLUMN_GROUP, 0, 0)
    source_dual, target_dual = pl.pallas_call(
        last_kernel,
        out_shape=(whole_rows, whole_rows),
        in_specs=[VMEM] * 4,
        out_specs=(VMEM, VMEM),
        scratch_shapes=[pltpu.VMEM((blocks, size), jnp.float32)],
        compiler_params=PARAMS,
        name="last",
    )(parts, tgt_weight.reshape(blocks, size), mine, other)
    return (source_dual.reshape(-1), target_dual.reshape(-1))


def solution(mesh):
    fine = Mesh(mesh.devices.reshape(tuple(SRC.values()) + tuple(TGT.values())), tuple(SRC) + tuple(TGT))
    src, tgt = tuple(SRC), tuple(TGT)
    placed = (P(src + tgt, None), P(tgt + src, None), P(src), P(tgt), P(src, tgt, None), P(src, tgt))
    return jax.shard_map(
        on_device, mesh=fine, in_specs=placed, out_specs=(P(src), P(tgt)), check_vma=False
    )
```

```python
import functools
import math

import jax
import jax.numpy as jnp
from jax import lax
from jax.experimental import pallas as pl
from jax.experimental.pallas import tpu as pltpu
from jax.sharding import Mesh
from jax.sharding import PartitionSpec as P

ITERS = 3
UNROLL = 8
FIELDS = 5
LOW = -1e30
LN2 = math.log(2.0)
LOG2E = math.log2(math.e)

SRC = {"x": 4, "l": 2, "c": 2}
TGT = {"z": 8, "h": 2}
ROW_GROUP = ("z", "c")
COLUMN_GROUP = ("x", "l", "h")
LAST_GROUP = ("x", "l", "c", "h")
PIECES = (8,)

VMEM = pl.BlockSpec(memory_space=pltpu.VMEM)
SMEM = pl.BlockSpec(memory_space=pltpu.SMEM)
ANY = pl.BlockSpec(memory_space=pl.ANY)
PARAMS = pltpu.CompilerParams(vmem_limit_bytes=8 * 1024 * 1024)


def arrival(stages):
    offsets = [0]
    for hop in range(1, stages // 2):
        offsets += [-hop, hop]
    return offsets + [stages // 2]


def prepare_kernel(slots, own_hbm, tgt_hbm, *refs):
    lists_hbm, whole_ref, held_ref, tgt_ref, info_ref, refs, sems = refs[:4], *refs[4:8], refs[8:-1], refs[-1]
    pairs = ((tgt_hbm, tgt_ref), (own_hbm, held_ref)) + tuple(zip(lists_hbm, refs))
    moves = [pltpu.make_async_copy(source, target, sems.at[n]) for n, (source, target) in enumerate(pairs)]
    for move in moves:
        move.start()
    info_ref[...] = jnp.zeros(info_ref.shape, jnp.float32)
    for move in moves:
        move.wait()
    for flip, (cand_ref, counts_ref) in enumerate((refs[:2], refs[2:])):
        blocks = cand_ref.shape[2]
        for slot in range(slots):
            info_ref[8 * flip + slot : 8 * flip + slot + 1, :blocks] = cand_ref[slot].astype(jnp.float32)
        info_ref[8 * flip + slots : 8 * flip + slots + 1, :blocks] = counts_ref[...].astype(jnp.float32)
    size = tgt_ref.shape[0]
    info = info_ref[...].astype(whole_ref.dtype)
    for part in range(whole_ref.shape[0]):
        whole_ref[part, :size, :] = tgt_ref[...]
        whole_ref[part, size:, :] = info


def plan_kernel(stages, slots, room, rows_ref, src_hbm, tgt_hbm, plan_ref, src_log_ref, tgt_log_ref, src_ref,
                tgt_ref, lists_ref, info_ref, sems):
    moves = (pltpu.make_async_copy(src_hbm, src_ref, sems.at[0]), pltpu.make_async_copy(tgt_hbm, tgt_ref, sems.at[1]))
    for move in moves:
        move.start()
    deep, side, core = lax.axis_index("z"), lax.axis_index("h"), lax.axis_index("c")
    pair = (lax.axis_index("x") * 2 + lax.axis_index("l")) * 2
    lanes = lists_ref.shape[1]
    size = rows_ref.shape[1] - 16
    for flip in range(2):
        rows = rows_ref[pair + (side + flip) % 2, size:, :lanes].astype(jnp.float32)
        lists_ref[16 * flip : 16 * flip + 16, :] = rows.astype(jnp.int32)
    fetch = pltpu.make_async_copy(lists_ref, info_ref, sems.at[2])
    fetch.start()
    fetch.wait()
    blocks = 2 * stages
    spare = blocks * blocks

    def put(at, block, target, row, column, place):
        for field, value in enumerate((block, target, row, column, place)):
            plan_ref[field * room + at] = value

    total = 0
    offsets = arrival(stages)
    chunk = 0
    for piece, length in enumerate(PIECES):
        plan_ref[FIELDS * room + piece] = total // UNROLL
        for place in range(2 * length):
            depth = (deep + offsets[chunk + place // 2] + stages) % stages
            first = 8 * (place % 2)
            block = depth * 2 + (core + place % 2) % 2
            row = depth * 2 + side
            for flip in range(2):

                def add(slot, at, first=first, flip=flip, row=row, block=block, place=place):
                    local = info_ref[16 * flip + first + slot, row]
                    target = local - local % 2 + (side + flip) % 2
                    put(at, block, target, target * blocks + block, block * blocks + target, place)
                    return at + jnp.where(local % 2 == core, 1, 0)

                total = lax.fori_loop(0, info_ref[16 * flip + first + slots, row], add, total)
        for extra in range(UNROLL - 1):
            put(total + extra, 0, 0, spare, spare, 0)
        total = (total + UNROLL - 1) // UNROLL * UNROLL
        chunk += length
    plan_ref[FIELDS * room + len(PIECES)] = total // UNROLL
    for move in moves:
        move.wait()
    for row in range(stages):
        src_log_ref[row : row + 1, :] = jnp.log2(src_ref[pl.ds(row * 2 + side, 1), :])
        tgt_log_ref[row : row + 1, :] = jnp.log2(tgt_ref[pl.ds(row * 2 + core, 1), :])


def clear(high_ref, total_ref):
    high_ref[...] = jnp.full(high_ref.shape, LOW, jnp.float32)
    total_ref[...] = jnp.zeros(total_ref.shape, jnp.float32)


def keep_stats(shifted, row, high_ref, total_ref):
    highest = jnp.max(shifted, axis=0, keepdims=True)
    high_ref[pl.ds(row, 1), :] = highest
    total_ref[pl.ds(row, 1), :] = jnp.sum(jnp.exp2(shifted - highest), axis=0, keepdims=True)


def local_lse(high_ref, total_ref, kept):
    outer = (high_ref.shape[0] - 8) // kept
    shape = (outer, kept, high_ref.shape[1])
    high = high_ref[: outer * kept, :].reshape(shape)
    total = total_ref[: outer * kept, :].reshape(shape)
    highest = jnp.max(high, axis=0)
    totals = jnp.sum(total * jnp.exp2(high - highest[None]), axis=0)
    return highest + jnp.log2(totals)


def copies(local, log_ref, out_ref):
    kept = local.shape[0]
    for part in range(out_ref.shape[0]):
        out_ref[part, :kept, :] = local
        if log_ref is not None:
            out_ref[part, kept:, :] = log_ref[...]


def potential(parts_ref, weight):
    parts = parts_ref[:, : weight.shape[0], :]
    highest = jnp.max(parts, axis=0)
    totals = jnp.sum(jnp.exp2(parts - highest[None]), axis=0)
    return weight - (highest + jnp.log2(totals))


def matmul(left, right, scale):
    return scale * lax.dot_general(
        left, right, (((1,), (1,)), ((), ())), preferred_element_type=jnp.float32)


def first_kernel(room, scale, piece, plan_ref, tgt_ref, *refs):
    count = 2 * PIECES[piece]
    features, refs = refs[:count], refs[count:]
    log_ref = earlier_ref = None
    if piece:
        earlier_ref, refs = refs[0], refs[3:]
    if piece == len(PIECES) - 1:
        log_ref, refs = refs[0], refs[1:]
    flipped_ref, scores_ref, out_ref, held_ref, high_ref, total_ref = refs
    for place, ref in enumerate(features):
        held_ref[place] = ref[...]
    clear(high_ref, total_ref)

    def group(step, carry):
        for lane in range(UNROLL):
            at = step * UNROLL + lane
            left, right = held_ref[plan_ref[4 * room + at]], tgt_ref[plan_ref[room + at], : held_ref.shape[1], :]
            flipped = matmul(right, left, scale)
            flipped_ref[at] = flipped
            scores_ref[at] = flipped.T
            keep_stats(flipped, plan_ref[2 * room + at], high_ref, total_ref)
        return carry

    bounds = FIELDS * room + piece
    lax.fori_loop(plan_ref[bounds], plan_ref[bounds + 1], group, 0)
    local = local_lse(high_ref, total_ref, out_ref.shape[0])
    if piece:
        local = jnp.maximum(local, earlier_ref[...])
    if log_ref is None:
        out_ref[...] = local
    else:
        copies(local, log_ref, out_ref)


def pass_kernel(room, own, row, fresh, first, emit, plan_ref, parts_ref, weight_ref, scores_ref, *refs):
    log_ref = weight_ref if first else None
    out_ref, refs = refs[0], refs[1:]
    if fresh:
        kept_ref, refs = refs[0], refs[1:]
        blocks = kept_ref.shape[0]
        for block in range(blocks):
            at = blocks + block // 2
            kept_ref[block : block + 1, :] = parts_ref[block % 2, at : at + 1, :]
        weight_ref = kept_ref
    column_ref, high_ref, total_ref = refs[:3]
    if emit:
        dual_ref = refs[3]
    dual = potential(parts_ref, weight_ref[...])
    blocks = dual.shape[0]
    if emit:
        high_ref[:blocks, :] = dual * LN2
        for block in range(blocks // 2):
            dual_ref[block : block + 1, :] = high_ref[pl.ds(2 * block + lax.axis_index("c"), 1), :]
    turned = dual.T
    for block in range(blocks):
        column_ref[block] = jnp.broadcast_to(turned[:, block : block + 1], column_ref.shape[1:])
    clear(high_ref, total_ref)

    def group(step, carry):
        for lane in range(UNROLL):
            at = step * UNROLL + lane
            shifted = scores_ref[at] + column_ref[plan_ref[own * room + at]]
            keep_stats(shifted, plan_ref[row * room + at], high_ref, total_ref)
        return carry

    lax.fori_loop(0, plan_ref[FIELDS * room + len(PIECES)], group, 0)
    local = local_lse(high_ref, total_ref, blocks)
    if not emit:
        copies(local, log_ref, out_ref)
        return
    for block in range(blocks):
        at = block % 2 * (blocks // 2) + block // 2
        high_ref[at : at + 1, :] = local[block : block + 1, :]
    for part in range(out_ref.shape[0]):
        out_ref[part, : blocks // 2, :] = high_ref[pl.ds(part % 2 * (blocks // 2), blocks // 2), :]
        out_ref[part, blocks // 2 :, :] = dual_ref[...]


def last_kernel(parts_ref, weight_ref, src_ref, tgt_ref, lse_ref):
    half = parts_ref.shape[1] // 2
    place = (lax.axis_index("x") * 2 + lax.axis_index("l")) * 2 + lax.axis_index("c")
    for side in range(2):
        for block in range(half):
            src_ref[2 * block + side : 2 * block + side + 1, :] = (
                parts_ref[2 * place + side, half + block : half + block + 1, :])
    for core in range(2):
        parts = [parts_ref[part, :half, :] for part in range(parts_ref.shape[0]) if part // 2 % 2 == core]
        highest = functools.reduce(jnp.maximum, parts)
        lse = highest + jnp.log2(sum(jnp.exp2(part - highest) for part in parts))
        for block in range(half):
            at = 2 * block + core
            lse_ref[at : at + 1, :] = lse[block : block + 1, :]
    tgt_ref[...] = (jnp.log2(weight_ref[...]) - lse_ref[...]) * LN2


def cost(pairs):
    return pl.CostEstimate(flops=pairs * 2 * 128 * 128 * 256, bytes_accessed=pairs * 65536, transcendentals=0)


def in_hbm(value):
    return pltpu.with_memory_space_constraint(value, pltpu.HBM)


def swap(value, axis):
    return lax.ppermute(value, axis, [(0, 1), (1, 0)])


def along_z(value, by):
    stages = lax.axis_size("z")
    return lax.ppermute(value, "z", [(k, (k + by) % stages) for k in range(stages)])


def on_device(src_feat, tgt_feat, src_weight, tgt_weight, cand, counts):
    slots = cand.shape[2]
    size, features = src_feat.shape
    stages = lax.axis_size("z")
    blocks = 2 * stages
    held = -(-2 * blocks * slots // UNROLL) * UNROLL + len(PIECES) * UNROLL
    room = -(-held // 128) * 128
    scale = LOG2E / math.sqrt(features)

    lists = (cand.transpose(2, 1, 0), counts.T)
    across = tuple(swap(part, "c") for part in lists)
    whole, own = pl.pallas_call(
        functools.partial(prepare_kernel, slots),
        out_shape=(
            jax.ShapeDtypeStruct((blocks, size + 16, features), tgt_feat.dtype),
            pltpu.VMEM(src_feat.shape, src_feat.dtype),
        ),
        in_specs=[ANY] * 6,
        out_specs=(VMEM, VMEM),
        scratch_shapes=[pltpu.VMEM(tgt_feat.shape, tgt_feat.dtype), pltpu.VMEM((16, features), jnp.float32)]
        + [pltpu.VMEM((slots, 1, blocks), jnp.int32), pltpu.VMEM((1, blocks), jnp.int32)] * 2
        + [pltpu.SemaphoreType.DMA((6,))],
        compiler_params=PARAMS,
        name="prepare",
    )(in_hbm(src_feat), in_hbm(tgt_feat), *map(in_hbm, lists), *across)
    with jax.named_scope("gather_features"):
        gated = (swap(src_feat, "c"), along_z(src_feat, 1), along_z(src_feat, -1))
        whole, other, up, down = lax.optimization_barrier((whole, *gated))
        target_rows = lax.all_to_all(whole, COLUMN_GROUP, 0, 0)
        chunks = [src_feat, up, down]
        for _ in range(2, stages // 2):
            up, down = along_z(up, 1), along_z(down, -1)
            chunks += [up, down]
        pairs = [own, other] + [part for chunk in chunks[1:] for part in (chunk, swap(chunk, "c"))]
        pairs += [along_z(up, 1), along_z(pairs[-1], -1)]

    half = jax.ShapeDtypeStruct((stages, size), jnp.float32)
    plan, src_log, tgt_log = pl.pallas_call(
        functools.partial(plan_kernel, stages, slots, room),
        out_shape=(pltpu.SMEM(((FIELDS + 1) * room,), jnp.int32), half, half),
        in_specs=[VMEM] + [ANY] * 2,
        out_specs=(SMEM, VMEM, VMEM),
        scratch_shapes=[pltpu.VMEM((blocks, size), jnp.float32)] * 2
        + [pltpu.VMEM((32, size), jnp.int32), pltpu.SMEM((32, size), jnp.int32), pltpu.SemaphoreType.DMA((3,))],
        compiler_params=PARAMS,
        name="plan",
    )(target_rows, in_hbm(src_weight.reshape(blocks, size)), in_hbm(tgt_weight.reshape(blocks, size)))
    plan = pltpu.with_memory_space_constraint(plan, pltpu.SMEM)

    tables = [pltpu.VMEM((blocks * blocks + 8, size), jnp.float32)] * 2
    tiles = pltpu.VMEM((held, size, size), jnp.float32)
    whole_rows = jax.ShapeDtypeStruct((blocks, size), jnp.float32)
    parts_of = lambda kept: jax.ShapeDtypeStruct((blocks, kept, size), jnp.float32)

    def first_rows(piece, some, local, scored, out, log, name):
        kept = [pltpu.with_memory_space_constraint(part, pltpu.VMEM) for part in scored]
        more = ([local] + kept if scored else []) + log
        given = 2 + len(some)
        *scored, local = pl.pallas_call(
            functools.partial(first_kernel, room, scale, piece),
            out_shape=(tiles, tiles, out),
            in_specs=[SMEM] + [VMEM] * (1 + len(some) + len(more)),
            out_specs=(VMEM, VMEM, VMEM),
            scratch_shapes=[pltpu.VMEM((len(some), size, features), src_feat.dtype)] + tables,
            input_output_aliases={given + 1: 0, given + 2: 1} if scored else {},
            compiler_params=PARAMS,
            cost_estimate=cost(5 * PIECES[piece]),
            name=name,
        )(plan, target_rows, *some, *more)
        return scored, local

    (flipped, scores), parts = first_rows(0, pairs, None, (), parts_of(blocks + stages), [src_log], "scores_and_rows")

    def sweep(own, row, step, emit, parts, weight, tiles, name):
        first, fresh = name == "columns" and not step, weight is None
        shapes = (parts_of(blocks + stages if first else blocks),)
        if emit:
            shapes = (jax.ShapeDtypeStruct((2 * blocks, blocks, size), jnp.float32),)
        shapes += (whole_rows,) * fresh
        weights = tgt_log if fresh else weight
        return pl.pallas_call(
            functools.partial(pass_kernel, room, own, row, fresh, first, emit),
            out_shape=shapes,
            in_specs=[SMEM, VMEM, VMEM, VMEM],
            out_specs=(VMEM,) * len(shapes),
            scratch_shapes=[pltpu.VMEM((blocks, size, size), jnp.float32)] + tables
            + [pltpu.VMEM((stages, size), jnp.float32)] * emit,
            compiler_params=PARAMS,
            name=name,
        )(plan, parts, weights, pltpu.with_memory_space_constraint(tiles, pltpu.VMEM))

    src_kept = tgt_kept = None
    for step in range(ITERS):
        if step:
            parts, *kept = sweep(1, 2, step, False, parts, tgt_kept, flipped, "rows")
            tgt_kept = kept[0] if kept else tgt_kept
        with jax.named_scope("exchange_rows"):
            parts = lax.all_to_all(parts, ROW_GROUP, 0, 0)
        last = step == ITERS - 1
        parts, *kept = sweep(0, 3, step, last, parts, src_kept, scores, "columns")
        src_kept = kept[0] if kept else src_kept
        with jax.named_scope("exchange_columns"):
            parts = lax.all_to_all(parts, LAST_GROUP if last else COLUMN_GROUP, 0, 0)
    source_dual, target_dual = pl.pallas_call(
        last_kernel,
        out_shape=(whole_rows, whole_rows),
        in_specs=[VMEM] * 2,
        out_specs=(VMEM, VMEM),
        scratch_shapes=[pltpu.VMEM((blocks, size), jnp.float32)],
        compiler_params=PARAMS,
        name="last",
    )(parts, tgt_weight.reshape(blocks, size))
    return (source_dual.reshape(-1), target_dual.reshape(-1))


def solution(mesh):
    fine = Mesh(mesh.devices.reshape(tuple(SRC.values()) + tuple(TGT.values())), tuple(SRC) + tuple(TGT))
    src, tgt = tuple(SRC), tuple(TGT)
    placed = (P(src + tgt, None), P(tgt + src, None), P(src), P(tgt), P(src, tgt, None), P(src, tgt))
    return jax.shard_map(
        on_device, mesh=fine, in_specs=placed, out_specs=(P(src), P(tgt)), check_vma=False
    )
```

```python
import functools
import math

import jax
import jax.numpy as jnp
from jax import lax
from jax.experimental import pallas as pl
from jax.experimental.pallas import tpu as pltpu
from jax.sharding import Mesh
from jax.sharding import PartitionSpec as P

ITERS = 3
UNROLL = 8
FIELDS = 5
LOW = -1e30
LN2 = math.log(2.0)
LOG2E = math.log2(math.e)

SRC = {"x": 4, "l": 2, "c": 2}
TGT = {"z": 8, "h": 2}
ROW_GROUP = ("z", "c")
COLUMN_GROUP = ("x", "l", "h")
LAST_GROUP = ("x", "l", "c", "h")
PIECES = (8,)

VMEM = pl.BlockSpec(memory_space=pltpu.VMEM)
SMEM = pl.BlockSpec(memory_space=pltpu.SMEM)
ANY = pl.BlockSpec(memory_space=pl.ANY)
PARAMS = pltpu.CompilerParams(vmem_limit_bytes=8 * 1024 * 1024)


def arrival(stages):
    offsets = [0]
    for hop in range(1, stages // 2):
        offsets += [-hop, hop]
    return offsets + [stages // 2]


def prepare_kernel(slots, own_hbm, tgt_hbm, *refs):
    lists_hbm, whole_ref, held_ref, near_ref, tgt_ref, info_ref, refs, sems = refs[:4], *refs[4:9], refs[9:-1], refs[-1]
    pairs = ((tgt_hbm, tgt_ref), (own_hbm, held_ref)) + tuple(zip(lists_hbm, refs))
    moves = [pltpu.make_async_copy(source, target, sems.at[n]) for n, (source, target) in enumerate(pairs)]
    for move in moves:
        move.start()
    info_ref[...] = jnp.zeros(info_ref.shape, jnp.float32)
    for move in moves:
        move.wait()
    for flip, (cand_ref, counts_ref) in enumerate((refs[:2], refs[2:])):
        blocks = cand_ref.shape[2]
        for slot in range(slots):
            info_ref[8 * flip + slot : 8 * flip + slot + 1, :blocks] = cand_ref[slot].astype(jnp.float32)
        info_ref[8 * flip + slots : 8 * flip + slots + 1, :blocks] = counts_ref[...].astype(jnp.float32)
    size = tgt_ref.shape[0]
    info = info_ref[...].astype(whole_ref.dtype)
    near_ref[...] = info_ref[...]
    for part in range(whole_ref.shape[0]):
        whole_ref[part, :size, :] = tgt_ref[...]
        whole_ref[part, size:, :] = info


def plan_kernel(stages, slots, room, flip, rows_ref, *refs):
    deep, side, core = lax.axis_index("z"), lax.axis_index("h"), lax.axis_index("c")
    plan_ref, lists_ref, info_ref, sem = (refs[0], *refs[-3:]) if flip else (refs[2], *refs[-3:])
    lanes = lists_ref.shape[1]
    if flip:
        pair = (lax.axis_index("x") * 2 + lax.axis_index("l")) * 2 + 1 - side
        rows = rows_ref[pair, rows_ref.shape[1] - 16 :, :lanes].astype(jnp.float32)
    else:
        rows = rows_ref[:, :lanes]
        for weight, out in zip(refs[:2], refs[3:5]):
            place = core if out is refs[4] else side
            for row in range(stages):
                out[row : row + 1, :] = jnp.log2(weight[pl.ds(row * 2 + place, 1), :])
    lists_ref[...] = rows.astype(jnp.int32)
    fetch = pltpu.make_async_copy(lists_ref, info_ref, sem)
    fetch.start()
    fetch.wait()
    blocks = 2 * stages
    spare = blocks * blocks

    def put(at, block, target, row, column, place):
        for field, value in enumerate((block, target, row, column, place)):
            plan_ref[field * room + at] = value

    total = 0
    offsets = arrival(stages)
    chunk = 0
    for piece, length in enumerate(PIECES):
        plan_ref[FIELDS * room + piece] = total // UNROLL
        for place in range(2 * length):
            depth = (deep + offsets[chunk + place // 2] + stages) % stages
            first = 8 * (place % 2)
            block = depth * 2 + (core + place % 2) % 2
            row = depth * 2 + side

            def add(slot, at, first=first, row=row, block=block, place=place):
                local = info_ref[first + slot, row]
                target = local - local % 2 + (side + flip) % 2
                put(at, block, target, target * blocks + block, block * blocks + target, place)
                return at + jnp.where(local % 2 == core, 1, 0)

            total = lax.fori_loop(0, info_ref[first + slots, row], add, total)
        for extra in range(UNROLL - 1):
            put(total + extra, 0, 0, spare, spare, 0)
        total = (total + UNROLL - 1) // UNROLL * UNROLL
        chunk += length
    plan_ref[FIELDS * room + len(PIECES)] = total // UNROLL


def both(near_ref, far_ref, end, group):
    count = near_ref[end]
    lax.fori_loop(0, count, functools.partial(group, near_ref, 0), 0)
    lax.fori_loop(0, far_ref[end], functools.partial(group, far_ref, count * UNROLL), 0)


def clear(high_ref, total_ref):
    high_ref[...] = jnp.full(high_ref.shape, LOW, jnp.float32)
    total_ref[...] = jnp.zeros(total_ref.shape, jnp.float32)


def keep_stats(shifted, row, high_ref, total_ref):
    highest = jnp.max(shifted, axis=0, keepdims=True)
    high_ref[pl.ds(row, 1), :] = highest
    total_ref[pl.ds(row, 1), :] = jnp.sum(jnp.exp2(shifted - highest), axis=0, keepdims=True)


def local_lse(high_ref, total_ref, kept):
    outer = (high_ref.shape[0] - 8) // kept
    shape = (outer, kept, high_ref.shape[1])
    high = high_ref[: outer * kept, :].reshape(shape)
    total = total_ref[: outer * kept, :].reshape(shape)
    highest = jnp.max(high, axis=0)
    totals = jnp.sum(total * jnp.exp2(high - highest[None]), axis=0)
    return highest + jnp.log2(totals)


def copies(local, log_ref, out_ref):
    kept = local.shape[0]
    for part in range(out_ref.shape[0]):
        out_ref[part, :kept, :] = local
        if log_ref is not None:
            out_ref[part, kept:, :] = log_ref[...]


def potential(parts_ref, weight):
    parts = parts_ref[:, : weight.shape[0], :]
    highest = jnp.max(parts, axis=0)
    totals = jnp.sum(jnp.exp2(parts - highest[None]), axis=0)
    return weight - (highest + jnp.log2(totals))


def matmul(left, right, scale):
    return scale * lax.dot_general(
        left, right, (((1,), (1,)), ((), ())), preferred_element_type=jnp.float32)


def first_kernel(room, scale, piece, near_ref, far_ref, tgt_ref, *refs):
    count = 2 * PIECES[piece]
    features, refs = refs[:count], refs[count:]
    log_ref = earlier_ref = None
    if piece:
        earlier_ref, refs = refs[0], refs[3:]
    if piece == len(PIECES) - 1:
        log_ref, refs = refs[0], refs[1:]
    flipped_ref, scores_ref, out_ref, held_ref, high_ref, total_ref = refs
    for place, ref in enumerate(features):
        held_ref[place] = ref[...]
    clear(high_ref, total_ref)

    def group(plan_ref, base, step, carry):
        for lane in range(UNROLL):
            at = step * UNROLL + lane
            tile = base + at
            left, right = held_ref[plan_ref[4 * room + at]], tgt_ref[plan_ref[room + at], : held_ref.shape[1], :]
            flipped = matmul(right, left, scale)
            flipped_ref[tile] = flipped
            scores_ref[tile] = flipped.T
            keep_stats(flipped, plan_ref[2 * room + at], high_ref, total_ref)
        return carry

    both(near_ref, far_ref, FIELDS * room + len(PIECES), group)
    local = local_lse(high_ref, total_ref, out_ref.shape[0])
    if piece:
        local = jnp.maximum(local, earlier_ref[...])
    if log_ref is None:
        out_ref[...] = local
    else:
        copies(local, log_ref, out_ref)


def pass_kernel(room, own, row, fresh, first, emit, near_ref, far_ref, parts_ref, weight_ref, scores_ref, *refs):
    log_ref = weight_ref if first else None
    out_ref, refs = refs[0], refs[1:]
    if fresh:
        kept_ref, refs = refs[0], refs[1:]
        blocks = kept_ref.shape[0]
        for block in range(blocks):
            at = blocks + block // 2
            kept_ref[block : block + 1, :] = parts_ref[block % 2, at : at + 1, :]
        weight_ref = kept_ref
    column_ref, high_ref, total_ref = refs[:3]
    if emit:
        dual_ref = refs[3]
    dual = potential(parts_ref, weight_ref[...])
    blocks = dual.shape[0]
    if emit:
        high_ref[:blocks, :] = dual * LN2
        for block in range(blocks // 2):
            dual_ref[block : block + 1, :] = high_ref[pl.ds(2 * block + lax.axis_index("c"), 1), :]
    turned = dual.T
    for block in range(blocks):
        column_ref[block] = jnp.broadcast_to(turned[:, block : block + 1], column_ref.shape[1:])
    clear(high_ref, total_ref)

    def group(plan_ref, base, step, carry):
        for lane in range(UNROLL):
            at = step * UNROLL + lane
            tile = base + at
            shifted = scores_ref[tile] + column_ref[plan_ref[own * room + at]]
            keep_stats(shifted, plan_ref[row * room + at], high_ref, total_ref)
        return carry

    both(near_ref, far_ref, FIELDS * room + len(PIECES), group)
    local = local_lse(high_ref, total_ref, blocks)
    if not emit:
        copies(local, log_ref, out_ref)
        return
    for block in range(blocks):
        at = block % 2 * (blocks // 2) + block // 2
        high_ref[at : at + 1, :] = local[block : block + 1, :]
    for part in range(out_ref.shape[0]):
        out_ref[part, : blocks // 2, :] = high_ref[pl.ds(part % 2 * (blocks // 2), blocks // 2), :]
        out_ref[part, blocks // 2 :, :] = dual_ref[...]


def last_kernel(parts_ref, weight_ref, src_ref, tgt_ref, lse_ref):
    half = parts_ref.shape[1] // 2
    place = (lax.axis_index("x") * 2 + lax.axis_index("l")) * 2 + lax.axis_index("c")
    for side in range(2):
        for block in range(half):
            src_ref[2 * block + side : 2 * block + side + 1, :] = (
                parts_ref[2 * place + side, half + block : half + block + 1, :])
    for core in range(2):
        parts = [parts_ref[part, :half, :] for part in range(parts_ref.shape[0]) if part // 2 % 2 == core]
        highest = functools.reduce(jnp.maximum, parts)
        lse = highest + jnp.log2(sum(jnp.exp2(part - highest) for part in parts))
        for block in range(half):
            at = 2 * block + core
            lse_ref[at : at + 1, :] = lse[block : block + 1, :]
    tgt_ref[...] = (jnp.log2(weight_ref[...]) - lse_ref[...]) * LN2


def cost(pairs):
    return pl.CostEstimate(flops=pairs * 2 * 128 * 128 * 256, bytes_accessed=pairs * 65536, transcendentals=0)


def in_hbm(value):
    return pltpu.with_memory_space_constraint(value, pltpu.HBM)


def swap(value, axis):
    return lax.ppermute(value, axis, [(0, 1), (1, 0)])


def along_z(value, by):
    stages = lax.axis_size("z")
    return lax.ppermute(value, "z", [(k, (k + by) % stages) for k in range(stages)])


def on_device(src_feat, tgt_feat, src_weight, tgt_weight, cand, counts):
    slots = cand.shape[2]
    size, features = src_feat.shape
    stages = lax.axis_size("z")
    blocks = 2 * stages
    held = -(-2 * blocks * slots // UNROLL) * UNROLL + 2 * UNROLL
    room = -(-held // 128) * 128
    scale = LOG2E / math.sqrt(features)

    lists = (cand.transpose(2, 1, 0), counts.T)
    across = tuple(swap(part, "c") for part in lists)
    whole, own, near = pl.pallas_call(
        functools.partial(prepare_kernel, slots),
        out_shape=(
            jax.ShapeDtypeStruct((blocks, size + 16, features), tgt_feat.dtype),
            pltpu.VMEM(src_feat.shape, src_feat.dtype),
            pltpu.VMEM((16, features), jnp.float32),
        ),
        in_specs=[ANY] * 6,
        out_specs=(VMEM, VMEM, VMEM),
        scratch_shapes=[pltpu.VMEM(tgt_feat.shape, tgt_feat.dtype), pltpu.VMEM((16, features), jnp.float32)]
        + [pltpu.VMEM((slots, 1, blocks), jnp.int32), pltpu.VMEM((1, blocks), jnp.int32)] * 2
        + [pltpu.SemaphoreType.DMA((6,))],
        compiler_params=PARAMS,
        name="prepare",
    )(in_hbm(src_feat), in_hbm(tgt_feat), *map(in_hbm, lists), *across)
    with jax.named_scope("gather_features"):
        gated = (swap(src_feat, "c"), along_z(src_feat, 1), along_z(src_feat, -1))
        whole, other, up, down = lax.optimization_barrier((whole, *gated))
        target_rows = lax.all_to_all(whole, COLUMN_GROUP, 0, 0)
        chunks = [src_feat, up, down]
        for _ in range(2, stages // 2):
            up, down = along_z(up, 1), along_z(down, -1)
            chunks += [up, down]
        pairs = [own, other] + [part for chunk in chunks[1:] for part in (chunk, swap(chunk, "c"))]
        pairs += [along_z(up, 1), along_z(pairs[-1], -1)]

    half = jax.ShapeDtypeStruct((stages, size), jnp.float32)
    listed = pltpu.SMEM(((FIELDS + 1) * room,), jnp.int32)
    lists = [pltpu.VMEM((16, size), jnp.int32), pltpu.SMEM((16, size), jnp.int32), pltpu.SemaphoreType.DMA]
    plan, src_log, tgt_log = pl.pallas_call(
        functools.partial(plan_kernel, stages, slots, room, 0),
        out_shape=(listed, half, half),
        in_specs=[VMEM] * 3,
        out_specs=(SMEM, VMEM, VMEM),
        scratch_shapes=lists,
        compiler_params=PARAMS,
        name="plan_near",
    )(near, src_weight.reshape(blocks, size), tgt_weight.reshape(blocks, size))
    plan_far = pl.pallas_call(
        functools.partial(plan_kernel, stages, slots, room, 1),
        out_shape=listed,
        in_specs=[VMEM],
        out_specs=SMEM,
        scratch_shapes=lists,
        compiler_params=PARAMS,
        name="plan_far",
    )(target_rows)
    plan, plan_far = (pltpu.with_memory_space_constraint(part, pltpu.SMEM) for part in (plan, plan_far))

    tables = [pltpu.VMEM((blocks * blocks + 8, size), jnp.float32)] * 2
    tiles = pltpu.VMEM((held, size, size), jnp.float32)
    whole_rows = jax.ShapeDtypeStruct((blocks, size), jnp.float32)
    parts_of = lambda kept: jax.ShapeDtypeStruct((blocks, kept, size), jnp.float32)

    def first_rows(piece, some, local, scored, out, log, name):
        kept = [pltpu.with_memory_space_constraint(part, pltpu.VMEM) for part in scored]
        more = ([local] + kept if scored else []) + log
        given = 2 + len(some)
        *scored, local = pl.pallas_call(
            functools.partial(first_kernel, room, scale, piece),
            out_shape=(tiles, tiles, out),
            in_specs=[SMEM] * 2 + [VMEM] * (1 + len(some) + len(more)),
            out_specs=(VMEM, VMEM, VMEM),
            scratch_shapes=[pltpu.VMEM((len(some), size, features), src_feat.dtype)] + tables,
            input_output_aliases={given + 1: 0, given + 2: 1} if scored else {},
            compiler_params=PARAMS,
            cost_estimate=cost(5 * PIECES[piece]),
            name=name,
        )(plan, plan_far, target_rows, *some, *more)
        return scored, local

    (flipped, scores), parts = first_rows(0, pairs, None, (), parts_of(blocks + stages), [src_log], "scores_and_rows")

    def sweep(own, row, step, emit, parts, weight, tiles, name):
        first, fresh = name == "columns" and not step, weight is None
        shapes = (parts_of(blocks + stages if first else blocks),)
        if emit:
            shapes = (jax.ShapeDtypeStruct((2 * blocks, blocks, size), jnp.float32),)
        shapes += (whole_rows,) * fresh
        weights = tgt_log if fresh else weight
        return pl.pallas_call(
            functools.partial(pass_kernel, room, own, row, fresh, first, emit),
            out_shape=shapes,
            in_specs=[SMEM, SMEM, VMEM, VMEM, VMEM],
            out_specs=(VMEM,) * len(shapes),
            scratch_shapes=[pltpu.VMEM((blocks, size, size), jnp.float32)] + tables
            + [pltpu.VMEM((stages, size), jnp.float32)] * emit,
            compiler_params=PARAMS,
            name=name,
        )(plan, plan_far, parts, weights, pltpu.with_memory_space_constraint(tiles, pltpu.VMEM))

    src_kept = tgt_kept = None
    for step in range(ITERS):
        if step:
            parts, *kept = sweep(1, 2, step, False, parts, tgt_kept, flipped, "rows")
            tgt_kept = kept[0] if kept else tgt_kept
        with jax.named_scope("exchange_rows"):
            parts = lax.all_to_all(parts, ROW_GROUP, 0, 0)
        last = step == ITERS - 1
        parts, *kept = sweep(0, 3, step, last, parts, src_kept, scores, "columns")
        src_kept = kept[0] if kept else src_kept
        with jax.named_scope("exchange_columns"):
            parts = lax.all_to_all(parts, LAST_GROUP if last else COLUMN_GROUP, 0, 0)
    source_dual, target_dual = pl.pallas_call(
        last_kernel,
        out_shape=(whole_rows, whole_rows),
        in_specs=[VMEM] * 2,
        out_specs=(VMEM, VMEM),
        scratch_shapes=[pltpu.VMEM((blocks, size), jnp.float32)],
        compiler_params=PARAMS,
        name="last",
    )(parts, tgt_weight.reshape(blocks, size))
    return (source_dual.reshape(-1), target_dual.reshape(-1))


def solution(mesh):
    fine = Mesh(mesh.devices.reshape(tuple(SRC.values()) + tuple(TGT.values())), tuple(SRC) + tuple(TGT))
    src, tgt = tuple(SRC), tuple(TGT)
    placed = (P(src + tgt, None), P(tgt + src, None), P(src), P(tgt), P(src, tgt, None), P(src, tgt))
    return jax.shard_map(
        on_device, mesh=fine, in_specs=placed, out_specs=(P(src), P(tgt)), check_vma=False
    )
```

```python
import functools
import math

import jax
import jax.numpy as jnp
from jax import lax
from jax.experimental import pallas as pl
from jax.experimental.pallas import tpu as pltpu
from jax.sharding import Mesh
from jax.sharding import PartitionSpec as P

ITERS = 3
UNROLL = 16
FIELDS = 5
LOW = -1e30
LN2 = math.log(2.0)
LOG2E = math.log2(math.e)

SRC = {"x": 4, "l": 2, "c": 2}
TGT = {"z": 8, "h": 2}
ROW_GROUP = ("z", "c")
COLUMN_GROUP = ("x", "l", "h")
LAST_GROUP = ("x", "l", "c", "h")
PIECES = (8,)

VMEM = pl.BlockSpec(memory_space=pltpu.VMEM)
SMEM = pl.BlockSpec(memory_space=pltpu.SMEM)
ANY = pl.BlockSpec(memory_space=pl.ANY)
PARAMS = pltpu.CompilerParams(vmem_limit_bytes=8 * 1024 * 1024)


def arrival(stages):
    offsets = [0]
    for hop in range(1, stages // 2):
        offsets += [-hop, hop]
    return offsets + [stages // 2]


def prepare_kernel(slots, own_hbm, tgt_hbm, *refs):
    lists_hbm, whole_ref, held_ref, tgt_ref, info_ref, refs, sems = refs[:4], *refs[4:8], refs[8:-1], refs[-1]
    pairs = ((tgt_hbm, tgt_ref), (own_hbm, held_ref)) + tuple(zip(lists_hbm, refs))
    moves = [pltpu.make_async_copy(source, target, sems.at[n]) for n, (source, target) in enumerate(pairs)]
    for move in moves:
        move.start()
    info_ref[...] = jnp.zeros(info_ref.shape, jnp.float32)
    for move in moves:
        move.wait()
    for flip, (cand_ref, counts_ref) in enumerate((refs[:2], refs[2:])):
        blocks = cand_ref.shape[2]
        for slot in range(slots):
            info_ref[8 * flip + slot : 8 * flip + slot + 1, :blocks] = cand_ref[slot].astype(jnp.float32)
        info_ref[8 * flip + slots : 8 * flip + slots + 1, :blocks] = counts_ref[...].astype(jnp.float32)
    size = tgt_ref.shape[0]
    info = info_ref[...].astype(whole_ref.dtype)
    for part in range(whole_ref.shape[0]):
        whole_ref[part, :size, :] = tgt_ref[...]
        whole_ref[part, size:, :] = info


def plan_kernel(stages, slots, room, rows_ref, src_hbm, tgt_hbm, plan_ref, src_log_ref, tgt_log_ref, src_ref,
                tgt_ref, lists_ref, info_ref, sems):
    moves = (pltpu.make_async_copy(src_hbm, src_ref, sems.at[0]), pltpu.make_async_copy(tgt_hbm, tgt_ref, sems.at[1]))
    for move in moves:
        move.start()
    deep, side, core = lax.axis_index("z"), lax.axis_index("h"), lax.axis_index("c")
    pair = (lax.axis_index("x") * 2 + lax.axis_index("l")) * 2
    lanes = lists_ref.shape[1]
    size = rows_ref.shape[1] - 16
    for flip in range(2):
        rows = rows_ref[pair + (side + flip) % 2, size:, :lanes].astype(jnp.float32)
        lists_ref[16 * flip : 16 * flip + 16, :] = rows.astype(jnp.int32)
    fetch = pltpu.make_async_copy(lists_ref, info_ref, sems.at[2])
    fetch.start()
    fetch.wait()
    blocks = 2 * stages
    spare = blocks * blocks

    def put(at, block, target, row, column, place):
        for field, value in enumerate((block, target, row, column, place)):
            plan_ref[field * room + at] = value

    total = 0
    offsets = arrival(stages)
    chunk = 0
    for piece, length in enumerate(PIECES):
        plan_ref[FIELDS * room + piece] = total // UNROLL
        for place in range(2 * length):
            depth = (deep + offsets[chunk + place // 2] + stages) % stages
            first = 8 * (place % 2)
            block = depth * 2 + (core + place % 2) % 2
            row = depth * 2 + side
            for flip in range(2):

                def add(slot, at, first=first, flip=flip, row=row, block=block, place=place):
                    local = info_ref[16 * flip + first + slot, row]
                    target = local - local % 2 + (side + flip) % 2
                    put(at, block, target, target * blocks + block, block * blocks + target, place)
                    return at + jnp.where(local % 2 == core, 1, 0)

                total = lax.fori_loop(0, info_ref[16 * flip + first + slots, row], add, total)
        for extra in range(UNROLL - 1):
            put(total + extra, 0, 0, spare, spare, 0)
        total = (total + UNROLL - 1) // UNROLL * UNROLL
        chunk += length
    plan_ref[FIELDS * room + len(PIECES)] = total // UNROLL
    for move in moves:
        move.wait()
    for row in range(stages):
        src_log_ref[row : row + 1, :] = jnp.log2(src_ref[pl.ds(row * 2 + side, 1), :])
        tgt_log_ref[row : row + 1, :] = jnp.log2(tgt_ref[pl.ds(row * 2 + core, 1), :])


def clear(high_ref, total_ref):
    high_ref[...] = jnp.full(high_ref.shape, LOW, jnp.float32)
    total_ref[...] = jnp.zeros(total_ref.shape, jnp.float32)


def keep_stats(shifted, row, high_ref, total_ref):
    highest = jnp.max(shifted, axis=0, keepdims=True)
    high_ref[pl.ds(row, 1), :] = highest
    total_ref[pl.ds(row, 1), :] = jnp.sum(jnp.exp2(shifted - highest), axis=0, keepdims=True)


def local_lse(high_ref, total_ref, kept):
    outer = (high_ref.shape[0] - 8) // kept
    shape = (outer, kept, high_ref.shape[1])
    high = high_ref[: outer * kept, :].reshape(shape)
    total = total_ref[: outer * kept, :].reshape(shape)
    highest = jnp.max(high, axis=0)
    totals = jnp.sum(total * jnp.exp2(high - highest[None]), axis=0)
    return highest + jnp.log2(totals)


def copies(local, log_ref, out_ref):
    kept = local.shape[0]
    for part in range(out_ref.shape[0]):
        out_ref[part, :kept, :] = local
        if log_ref is not None:
            out_ref[part, kept:, :] = log_ref[...]


def potential(parts_ref, weight):
    parts = parts_ref[:, : weight.shape[0], :]
    highest = jnp.max(parts, axis=0)
    totals = jnp.sum(jnp.exp2(parts - highest[None]), axis=0)
    return weight - (highest + jnp.log2(totals))


def matmul(left, right, scale):
    return scale * lax.dot_general(
        left, right, (((1,), (1,)), ((), ())), preferred_element_type=jnp.float32)


def first_kernel(room, scale, piece, plan_ref, tgt_ref, *refs):
    count = 2 * PIECES[piece]
    features, refs = refs[:count], refs[count:]
    log_ref = earlier_ref = None
    if piece:
        earlier_ref, refs = refs[0], refs[3:]
    if piece == len(PIECES) - 1:
        log_ref, refs = refs[0], refs[1:]
    flipped_ref, scores_ref, out_ref, held_ref, high_ref, total_ref = refs
    for place, ref in enumerate(features):
        held_ref[place] = ref[...]
    clear(high_ref, total_ref)

    def group(step, carry):
        for lane in range(UNROLL):
            at = step * UNROLL + lane
            left, right = held_ref[plan_ref[4 * room + at]], tgt_ref[plan_ref[room + at], : held_ref.shape[1], :]
            flipped = matmul(right, left, scale)
            flipped_ref[at] = flipped
            scores_ref[at] = flipped.T
            keep_stats(flipped, plan_ref[2 * room + at], high_ref, total_ref)
        return carry

    bounds = FIELDS * room + piece
    lax.fori_loop(plan_ref[bounds], plan_ref[bounds + 1], group, 0)
    local = local_lse(high_ref, total_ref, out_ref.shape[0])
    if piece:
        local = jnp.maximum(local, earlier_ref[...])
    if log_ref is None:
        out_ref[...] = local
    else:
        copies(local, log_ref, out_ref)


def pass_kernel(room, own, row, fresh, first, emit, plan_ref, parts_ref, weight_ref, scores_ref, *refs):
    log_ref = weight_ref if first else None
    out_ref, refs = refs[0], refs[1:]
    if fresh:
        kept_ref, refs = refs[0], refs[1:]
        blocks = kept_ref.shape[0]
        for block in range(blocks):
            at = blocks + block // 2
            kept_ref[block : block + 1, :] = parts_ref[block % 2, at : at + 1, :]
        weight_ref = kept_ref
    column_ref, high_ref, total_ref = refs[:3]
    if emit:
        dual_ref = refs[3]
    dual = potential(parts_ref, weight_ref[...])
    blocks = dual.shape[0]
    if emit:
        high_ref[:blocks, :] = dual * LN2
        for block in range(blocks // 2):
            dual_ref[block : block + 1, :] = high_ref[pl.ds(2 * block + lax.axis_index("c"), 1), :]
    turned = dual.T
    for block in range(blocks):
        column_ref[block] = jnp.broadcast_to(turned[:, block : block + 1], column_ref.shape[1:])
    clear(high_ref, total_ref)

    def group(step, carry):
        for lane in range(UNROLL):
            at = step * UNROLL + lane
            shifted = scores_ref[at] + column_ref[plan_ref[own * room + at]]
            keep_stats(shifted, plan_ref[row * room + at], high_ref, total_ref)
        return carry

    lax.fori_loop(0, plan_ref[FIELDS * room + len(PIECES)], group, 0)
    local = local_lse(high_ref, total_ref, blocks)
    if not emit:
        copies(local, log_ref, out_ref)
        return
    for block in range(blocks):
        at = block % 2 * (blocks // 2) + block // 2
        high_ref[at : at + 1, :] = local[block : block + 1, :]
    for part in range(out_ref.shape[0]):
        out_ref[part, : blocks // 2, :] = high_ref[pl.ds(part % 2 * (blocks // 2), blocks // 2), :]
        out_ref[part, blocks // 2 :, :] = dual_ref[...]


def last_kernel(parts_ref, weight_ref, src_ref, tgt_ref, lse_ref):
    half = parts_ref.shape[1] // 2
    place = (lax.axis_index("x") * 2 + lax.axis_index("l")) * 2 + lax.axis_index("c")
    for side in range(2):
        for block in range(half):
            src_ref[2 * block + side : 2 * block + side + 1, :] = (
                parts_ref[2 * place + side, half + block : half + block + 1, :])
    for core in range(2):
        parts = [parts_ref[part, :half, :] for part in range(parts_ref.shape[0]) if part // 2 % 2 == core]
        highest = functools.reduce(jnp.maximum, parts)
        lse = highest + jnp.log2(sum(jnp.exp2(part - highest) for part in parts))
        for block in range(half):
            at = 2 * block + core
            lse_ref[at : at + 1, :] = lse[block : block + 1, :]
    tgt_ref[...] = (jnp.log2(weight_ref[...]) - lse_ref[...]) * LN2


def cost(pairs):
    return pl.CostEstimate(flops=pairs * 2 * 128 * 128 * 256, bytes_accessed=pairs * 65536, transcendentals=0)


def in_hbm(value):
    return pltpu.with_memory_space_constraint(value, pltpu.HBM)


def swap(value, axis):
    return lax.ppermute(value, axis, [(0, 1), (1, 0)])


def along_z(value, by):
    stages = lax.axis_size("z")
    return lax.ppermute(value, "z", [(k, (k + by) % stages) for k in range(stages)])


def on_device(src_feat, tgt_feat, src_weight, tgt_weight, cand, counts):
    slots = cand.shape[2]
    size, features = src_feat.shape
    stages = lax.axis_size("z")
    blocks = 2 * stages
    held = -(-2 * blocks * slots // UNROLL) * UNROLL + len(PIECES) * UNROLL
    room = -(-held // 128) * 128
    scale = LOG2E / math.sqrt(features)

    lists = (cand.transpose(2, 1, 0), counts.T)
    across = tuple(swap(part, "c") for part in lists)
    whole, own = pl.pallas_call(
        functools.partial(prepare_kernel, slots),
        out_shape=(
            jax.ShapeDtypeStruct((blocks, size + 16, features), tgt_feat.dtype),
            pltpu.VMEM(src_feat.shape, src_feat.dtype),
        ),
        in_specs=[ANY] * 6,
        out_specs=(VMEM, VMEM),
        scratch_shapes=[pltpu.VMEM(tgt_feat.shape, tgt_feat.dtype), pltpu.VMEM((16, features), jnp.float32)]
        + [pltpu.VMEM((slots, 1, blocks), jnp.int32), pltpu.VMEM((1, blocks), jnp.int32)] * 2
        + [pltpu.SemaphoreType.DMA((6,))],
        compiler_params=PARAMS,
        name="prepare",
    )(in_hbm(src_feat), in_hbm(tgt_feat), *map(in_hbm, lists), *across)
    with jax.named_scope("gather_features"):
        gated = (swap(src_feat, "c"), along_z(src_feat, 1), along_z(src_feat, -1))
        whole, other, up, down = lax.optimization_barrier((whole, *gated))
        target_rows = lax.all_to_all(whole, COLUMN_GROUP, 0, 0)
        chunks = [src_feat, up, down]
        for _ in range(2, stages // 2):
            up, down = along_z(up, 1), along_z(down, -1)
            chunks += [up, down]
        pairs = [own, other] + [part for chunk in chunks[1:] for part in (chunk, swap(chunk, "c"))]
        pairs += [along_z(up, 1), along_z(pairs[-1], -1)]

    half = jax.ShapeDtypeStruct((stages, size), jnp.float32)
    plan, src_log, tgt_log = pl.pallas_call(
        functools.partial(plan_kernel, stages, slots, room),
        out_shape=(pltpu.SMEM(((FIELDS + 1) * room,), jnp.int32), half, half),
        in_specs=[VMEM] + [ANY] * 2,
        out_specs=(SMEM, VMEM, VMEM),
        scratch_shapes=[pltpu.VMEM((blocks, size), jnp.float32)] * 2
        + [pltpu.VMEM((32, size), jnp.int32), pltpu.SMEM((32, size), jnp.int32), pltpu.SemaphoreType.DMA((3,))],
        compiler_params=PARAMS,
        name="plan",
    )(target_rows, in_hbm(src_weight.reshape(blocks, size)), in_hbm(tgt_weight.reshape(blocks, size)))
    plan = pltpu.with_memory_space_constraint(plan, pltpu.SMEM)

    tables = [pltpu.VMEM((blocks * blocks + 8, size), jnp.float32)] * 2
    tiles = pltpu.VMEM((held, size, size), jnp.float32)
    whole_rows = jax.ShapeDtypeStruct((blocks, size), jnp.float32)
    parts_of = lambda kept: jax.ShapeDtypeStruct((blocks, kept, size), jnp.float32)

    def first_rows(piece, some, local, scored, out, log, name):
        kept = [pltpu.with_memory_space_constraint(part, pltpu.VMEM) for part in scored]
        more = ([local] + kept if scored else []) + log
        given = 2 + len(some)
        *scored, local = pl.pallas_call(
            functools.partial(first_kernel, room, scale, piece),
            out_shape=(tiles, tiles, out),
            in_specs=[SMEM] + [VMEM] * (1 + len(some) + len(more)),
            out_specs=(VMEM, VMEM, VMEM),
            scratch_shapes=[pltpu.VMEM((len(some), size, features), src_feat.dtype)] + tables,
            input_output_aliases={given + 1: 0, given + 2: 1} if scored else {},
            compiler_params=PARAMS,
            cost_estimate=cost(5 * PIECES[piece]),
            name=name,
        )(plan, target_rows, *some, *more)
        return scored, local

    (flipped, scores), parts = first_rows(0, pairs, None, (), parts_of(blocks + stages), [src_log], "scores_and_rows")

    def sweep(own, row, step, emit, parts, weight, tiles, name):
        first, fresh = name == "columns" and not step, weight is None
        shapes = (parts_of(blocks + stages if first else blocks),)
        if emit:
            shapes = (jax.ShapeDtypeStruct((2 * blocks, blocks, size), jnp.float32),)
        shapes += (whole_rows,) * fresh
        weights = tgt_log if fresh else weight
        return pl.pallas_call(
            functools.partial(pass_kernel, room, own, row, fresh, first, emit),
            out_shape=shapes,
            in_specs=[SMEM, VMEM, VMEM, VMEM],
            out_specs=(VMEM,) * len(shapes),
            scratch_shapes=[pltpu.VMEM((blocks, size, size), jnp.float32)] + tables
            + [pltpu.VMEM((stages, size), jnp.float32)] * emit,
            compiler_params=PARAMS,
            name=name,
        )(plan, parts, weights, pltpu.with_memory_space_constraint(tiles, pltpu.VMEM))

    src_kept = tgt_kept = None
    for step in range(ITERS):
        if step:
            parts, *kept = sweep(1, 2, step, False, parts, tgt_kept, flipped, "rows")
            tgt_kept = kept[0] if kept else tgt_kept
        with jax.named_scope("exchange_rows"):
            parts = lax.all_to_all(parts, ROW_GROUP, 0, 0)
        last = step == ITERS - 1
        parts, *kept = sweep(0, 3, step, last, parts, src_kept, scores, "columns")
        src_kept = kept[0] if kept else src_kept
        with jax.named_scope("exchange_columns"):
            parts = lax.all_to_all(parts, LAST_GROUP if last else COLUMN_GROUP, 0, 0)
    source_dual, target_dual = pl.pallas_call(
        last_kernel,
        out_shape=(whole_rows, whole_rows),
        in_specs=[VMEM] * 2,
        out_specs=(VMEM, VMEM),
        scratch_shapes=[pltpu.VMEM((blocks, size), jnp.float32)],
        compiler_params=PARAMS,
        name="last",
    )(parts, tgt_weight.reshape(blocks, size))
    return (source_dual.reshape(-1), target_dual.reshape(-1))


def solution(mesh):
    fine = Mesh(mesh.devices.reshape(tuple(SRC.values()) + tuple(TGT.values())), tuple(SRC) + tuple(TGT))
    src, tgt = tuple(SRC), tuple(TGT)
    placed = (P(src + tgt, None), P(tgt + src, None), P(src), P(tgt), P(src, tgt, None), P(src, tgt))
    return jax.shard_map(
        on_device, mesh=fine, in_specs=placed, out_specs=(P(src), P(tgt)), check_vma=False
    )
```
